128 devices in a mesh: elem: 32 (over y, x, core), blk: 4 (over z).
Axes of the slice: x: 4, y: 4, z: 4, core: 2. Of those that a mesh axis runs over, the one named last changes fastest.
Arguments:
- state: float32 [2048, 128, 4, 128], P('elem', 'blk'), may hold values from -6 to 6
- wind_x: float32 [2048, 128, 128], P('elem', 'blk'), may hold values from -6 to 6
- wind_y: float32 [2048, 128, 128], P('elem', 'blk'), may hold values from -6 to 6
- mixing: float32 [128, 128], replicated, may hold values from -1 to 0.92
- triggers: int32 [2048, 128], P('elem', 'blk'), may hold values 0 or 1
- group_costs: int32 [16384], P(('elem', 'blk')), may hold values from 1 to 64, as said below
- destinations: int32 [16384], P(('elem', 'blk')), may hold values from 0 to 127, as said below
Outputs:
- new_state: float32 [2048, 128, 4, 128], P('elem', 'blk')
- precipitation: float32 [262144], P(('elem', 'blk'))
The draws below stay inside these ranges and needn't reach their ends.
Inputs may be any that keep to these rules, and one draw needn't show every extreme that they name: `destinations`: every device is the destination of exactly 128 groups, at most 2 groups of one device go to one device, and some pair of devices reaches 2. `group_costs`: some group reaches 64.
All inputs are finite; a program needn't handle non-finite values. No bound on the sum of `triggers` on one device may be relied on, other than what follows from the above.
Results may differ from the reference program's by a relative error of at most 0.0001.
Values sent between devices are 32-bit elements; how exact they have to be, the bound alone decides.
No kernel may reach another device: no remote copies, remote signals or barrier semaphores. Data moves between devices by JAX's collectives and lax.ppermute only.
A program may use at most 128 MiB of HBM per device.

```python
import math
import jax
import jax.numpy as jnp
import numpy as np
from jax import lax

NT = 4
LEV = 128
NP = 4
GROUP_COLS = 16
MAXC = 64
PX = 64
PY = 32
GROUPS_DEV = 128
NX = 2048
NY = 128
N_ELEM = 32
N_BLK = 4
DEVICES = 128


def draw_mixing(key, part):
    key = jax.random.fold_in(key, 13)
    key_diag, key_off = jax.random.split(key)
    diagonal = jax.random.uniform(key_diag, (LEV,), jnp.float32, 0.8, 0.92)
    offdiag = jnp.clip(jax.random.normal(key_off, (LEV, LEV), jnp.float32), -4.0, 4.0)
    offdiag = offdiag * (0.1 / math.sqrt(LEV))
    identity = jnp.eye(LEV, dtype=jnp.float32)
    return offdiag * (1.0 - identity) + identity * diagonal[:, None]


def draw_group_costs(key, part):
    key = jax.random.fold_in(key, 12)
    key_ceil, key_count, key_pick = jax.random.split(key, 3)
    ceiling = jax.random.randint(key_ceil, (DEVICES, 1), 1, MAXC + 1)
    counts = jax.random.randint(key_count, (DEVICES, GROUPS_DEV), 1, ceiling + 1)
    picked = jax.random.randint(key_pick, (), 0, DEVICES)
    counts = counts.at[picked, 0].set(MAXC)
    return counts.reshape(-1).astype(jnp.int32)


def draw_destinations(key, part):
    key = jax.random.fold_in(key, 11)
    key_perm, key_rot = jax.random.split(key)
    share = GROUPS_DEV // DEVICES
    index = jnp.arange(DEVICES)
    pattern = jnp.where(index < DEVICES // 2, jnp.where(index % 2 == 0, 2 * share, 0), share).astype(jnp.int32)
    values = jax.random.permutation(key_perm, DEVICES).astype(jnp.int32)
    shifts = jnp.repeat(values, pattern, total_repeat_length=GROUPS_DEV)
    rotation = jax.random.randint(key_rot, (DEVICES,), 0, GROUPS_DEV)
    column = jnp.arange(GROUPS_DEV)
    picked = shifts[(column[None, :] + rotation[:, None]) % GROUPS_DEV]
    result = (index[:, None] + picked) % DEVICES
    return result.reshape(-1).astype(jnp.int32)


def plant(values, key, smallest, top_value):
    index_at = [jax.random.randint(jax.random.fold_in(key, axis), (), 0, length) for axis, length in enumerate(values.shape)]
    widest = values.shape.index(max(values.shape))
    neighbour = index_at[:widest] + [(index_at[widest] + 1) % values.shape[widest]] + index_at[widest + 1:]
    return values.at[tuple(index_at)].set(smallest).at[tuple(neighbour)].set(top_value)


def level_of(own_key, dims, cuts, smallest, top_value):
    def one(position, shards_of):
        heights = jax.random.uniform(jax.random.fold_in(jax.random.fold_in(own_key, 6), position), (shards_of,), jnp.float32, smallest / len(cuts), top_value / len(cuts))
        return jnp.repeat(jnp.exp(heights), dims[position] // shards_of).reshape((-1,) + (1,) * (len(dims) - position - 1))

    factor_of = one(*cuts[0])
    for cut in cuts[1:]:
        factor_of = factor_of * one(*cut)
    return factor_of


def bell_draw(rng, shape, spread, bound, cuts=(), held_as=jnp.bfloat16):
    loudness = level_of(rng, shape, cuts, -0.22, 0.18) if cuts else 1.0
    drawn = jax.random.normal(rng, shape, jnp.float32) * spread * loudness
    return jnp.minimum(jnp.maximum(drawn, -bound), bound).astype(held_as)


def setup_inputs(seed: int = 0) -> dict:
    key_list = jax.random.split(jax.random.key(seed), 8)
    return {
        "state": bell_draw(key_list[0], (NX, NY, NT, LEV), 1.0, 6.0, ((0, 32), (1, 4)), jnp.float32),
        "wind_x": bell_draw(key_list[1], (NX, NY, LEV), 1.0, 6.0, ((0, 32), (1, 4)), jnp.float32),
        "wind_y": bell_draw(key_list[2], (NX, NY, LEV), 1.0, 6.0, ((0, 32), (1, 4)), jnp.float32),
        "mixing": draw_mixing(jax.random.fold_in(key_list[7], 71), 0),
        "triggers": plant((jax.random.randint(key_list[4], (NX, NY), 0, 2) < 1).astype(jnp.int32), jax.random.fold_in(key_list[4], 1), 0, 1),
        "group_costs": draw_group_costs(jax.random.fold_in(key_list[7], 71), 0),
        "destinations": draw_destinations(jax.random.fold_in(key_list[7], 71), 0),
    }


def gll_derivative():
    gll_nodes = np.array([-1.0, -1.0 / np.sqrt(5.0), 1.0 / np.sqrt(5.0), 1.0])
    legendre = (5.0 * gll_nodes * gll_nodes * gll_nodes - 3.0 * gll_nodes) / 2.0
    derivative = np.zeros((4, 4))
    for a in range(4):
        for b in range(4):
            if a != b:
                derivative[a, b] = legendre[a] / (legendre[b] * (gll_nodes[a] - gll_nodes[b]))
    derivative[0, 0] = -3.0
    derivative[3, 3] = 3.0
    return jnp.asarray(derivative, jnp.float32)

def advect(state, wind_x, wind_y):
    deriv = gll_derivative()
    sizex, sizey, ntr, lev = state.shape
    along_x = jnp.einsum('ab,ebytl->eaytl', deriv, state.reshape(sizex // NP, NP, sizey, ntr, lev), precision=lax.Precision.HIGHEST).reshape(state.shape)
    along_y = jnp.einsum('ab,xebtl->xeatl', deriv, state.reshape(sizex, sizey // NP, NP, ntr, lev), precision=lax.Precision.HIGHEST).reshape(state.shape)
    return -0.05 * (wind_x[:, :, None, :] * along_x + wind_y[:, :, None, :] * along_y)

def reference(state, wind_x, wind_y, mixing, triggers, group_costs, destinations):
    tendency = advect(state, wind_x, wind_y)
    position_x = (jnp.arange(NX) % NP)[:, None, None, None]
    left_x = jnp.roll(tendency, 1, 0)
    right_x = jnp.roll(tendency, -1, 0)
    along_x = jnp.where(position_x == 0, (tendency + left_x) * 0.5, jnp.where(position_x == NP - 1, (tendency + right_x) * 0.5, tendency))
    position_y = (jnp.arange(NY) % NP)[None, :, None, None]
    left_y = jnp.roll(along_x, 1, 1)
    right_y = jnp.roll(along_x, -1, 1)
    smoothed = jnp.where(position_y == 0, (along_x + left_y) * 0.5, jnp.where(position_y == NP - 1, (along_x + right_y) * 0.5, along_x))
    advanced = state + smoothed
    columns = advanced.reshape(N_ELEM, PX, N_BLK, PY, NT, LEV).transpose(0, 2, 1, 3, 4, 5)
    columns = columns.reshape(DEVICES * GROUPS_DEV, GROUP_COLS, NT, LEV)
    trig_groups = triggers.reshape(N_ELEM, PX, N_BLK, PY).transpose(0, 2, 1, 3).reshape(DEVICES * GROUPS_DEV, GROUP_COLS)
    effort = trig_groups * group_costs[:, None]
    finished = columns
    for k in range(MAXC):
        remixed = jnp.einsum('sjtl,ml->sjtm', finished, mixing, precision=lax.Precision.HIGHEST)
        finished = jnp.where((effort > k)[:, :, None, None], remixed, finished)
    rain = lax.optimization_barrier(jnp.sum(columns[:, :, 1, :] - finished[:, :, 1, :], axis=-1)) * 0.125
    ranking = jnp.argsort(destinations, stable=True).astype(jnp.int32)
    precipitation = rain[ranking].reshape(-1)
    new_state = finished.reshape(N_ELEM, N_BLK, PX, PY, NT, LEV).transpose(0, 2, 1, 3, 4, 5).reshape(NX, NY, NT, LEV)
    return (new_state, precipitation)
```

```python
import functools

import jax
import jax.numpy as jnp
import numpy as np
from jax import lax
from jax.experimental import pallas as pl
from jax.experimental.pallas import tpu as pltpu
from jax.sharding import PartitionSpec as P

NP = 4
NT = 4
LEV = 128
GROUP_COLS = 16
MAXC = 64
LIMIT = 1.0e3
F32 = jnp.float32
BF16 = jnp.bfloat16
MIB = 1024 * 1024


def gll_derivative():
    nodes = np.array([-1.0, -1.0 / np.sqrt(5.0), 1.0 / np.sqrt(5.0), 1.0])
    legendre = (5.0 * nodes * nodes * nodes - 3.0 * nodes) / 2.0
    derivative = np.zeros((4, 4))
    for a in range(4):
        for b in range(4):
            if a != b:
                derivative[a, b] = legendre[a] / (legendre[b] * (nodes[a] - nodes[b]))
    derivative[0, 0] = -3.0
    derivative[3, 3] = 3.0
    return derivative


def split2(x):
    high = x.astype(BF16)
    return high, (x - high.astype(F32)).astype(BF16)


def split3(x):
    high = x.astype(BF16)
    rest = x - high.astype(F32)
    mid = rest.astype(BF16)
    return high, mid, (rest - mid.astype(F32)).astype(BF16)


def mm(a, b):
    return jnp.dot(a, b, preferred_element_type=F32)


def exact_pick(onehot, values):
    high, mid, low = split3(values)
    return mm(onehot, high) + mm(onehot, mid) + mm(onehot, low)


def weights(high, mid, low):
    pair = jnp.concatenate([high, mid], axis=1)
    return jnp.concatenate([pair, pair], axis=0), jnp.concatenate([low, high], axis=0)


def precise(high, mid, low, first, second):
    one = mm(jnp.concatenate([high, mid], axis=1), first)
    two = mm(jnp.concatenate([high, low], axis=1), second)
    return one[:, :LEV] + (one[:, LEV:] + two)


def repeated(start, cost, first_ref, second_ref):
    return lax.fori_loop(0, cost, lambda i, c: precise(*split3(c), first_ref[...], second_ref[...]), start)


def iota(shape, dim):
    return lax.broadcasted_iota(jnp.int32, shape, dim)


def gains_kernel(mixing_ref, dest_ref, trig_ref, gain_ref, onehot_ref, mask_ref, first_ref, second_ref, bad_ref, sums):
    square = mixing_ref[...]
    worst = jnp.max(jnp.abs(square))
    first_ref[...], second_ref[...] = weights(*split3(square.T))
    sums[0:8] = jnp.broadcast_to(jnp.sum(square, axis=0, keepdims=True), (8, LEV))
    for k in (1, 2, 4, 8, 16, 32):
        parts = split3(square)
        pair = weights(*parts)
        rows = max(k, 8)
        grown = precise(*split3(sums[0:rows]), *pair)
        if k < 8:
            pick = iota((8, LEV), 0)
            merged = sums[0:8]
            for j in range(k):
                merged = jnp.where(pick == j + k, grown[j:j + 1], merged)
            sums[0:8] = merged
        else:
            sums[k:2 * k] = grown
        if k < 32:
            square = precise(*parts, *pair)
            worst = jnp.maximum(worst, jnp.max(jnp.abs(square)))
    gain_ref[...] = 1.0 - sums[...]
    bad_ref[0] = jnp.where(worst <= LIMIT, 0, 1).astype(jnp.int32)

    groups = dest_ref.shape[1]
    shape = (groups, groups)
    dest_row = jnp.broadcast_to(dest_ref[...], shape)
    diagonal = iota(shape, 0) == iota(shape, 1)
    dest_col = jnp.sum(jnp.where(diagonal, dest_row, 0), axis=1, keepdims=True)
    earlier = (dest_col == dest_row) & (iota(shape, 0) < iota(shape, 1))
    within = jnp.sum(jnp.where(earlier, 1, 0), axis=0, keepdims=True)
    at = dest_row == iota(shape, 0)
    onehot_ref[0] = jnp.where(at & (within == 0), 1.0, 0.0).astype(BF16)
    onehot_ref[1] = jnp.where(at & (within == 1), 1.0, 0.0).astype(BF16)

    px, py = trig_ref.shape
    rows = py * NT
    trig = jnp.concatenate([trig_ref[...].astype(F32), jnp.zeros((LEV - px, py), F32)], axis=0).T
    spread = jnp.where(iota((rows, py), 0) // NT == iota((rows, py), 1), 1.0, 0.0).astype(BF16)
    mask_ref[...] = mm(spread, trig.astype(BF16))


def half_coefs(first, second):
    return jnp.where(iota((8, LEV), 0) < 4, F32(first), F32(second))


def derivative_tables():
    deriv = -0.05 * gll_derivative()
    g = [[float(np.float32(deriv[a, b])) for b in range(4)] for a in range(4)]
    low = [half_coefs(g[0][0], g[1][1]), half_coefs(g[0][1], g[1][0]), half_coefs(g[0][2], g[1][3]), half_coefs(g[0][3], g[1][2])]
    high = [half_coefs(g[2][0], g[3][1]), half_coefs(g[2][1], g[3][0]), half_coefs(g[2][2], g[3][3]), half_coefs(g[2][3], g[3][2])]
    return g, low, high


def tendency(k, points, load, load_x, load_y, store):
    g, low, high = derivative_tables()
    lower = iota((8, LEV), 0) < 4
    v = [[load(a, 16 * k + 8 * h) for h in range(2)] for a in range(NP)]
    for a in points:
        r = [pltpu.roll(v[a][h], 4, axis=0) for h in range(2)]
        for h, coefs in ((0, low), (1, high)):
            along_y = (coefs[0] * v[a][0] + coefs[1] * r[0]) + (coefs[2] * v[a][1] + coefs[3] * r[1])
            along_x = (g[a][0] * v[0][h] + g[a][1] * v[1][h]) + (g[a][2] * v[2][h] + g[a][3] * v[3][h])
            y = 4 * k + 2 * h
            wx = jnp.where(lower, load_x(a, y), load_x(a, y + 1))
            wy = jnp.where(lower, load_y(a, y), load_y(a, y + 1))
            store(a, 16 * k + 8 * h, wx * along_x + wy * along_y)


def sides_kernel(par_ref, low_ref, high_ref, low_x_ref, high_x_ref, low_y_ref, high_y_ref, send_a_ref, send_b_ref, first_ref, final_ref):
    even = par_ref[0] == 0
    for k in range(low_ref.shape[1] // 16):
        for ref, x_ref, y_ref, out_ref, at in ((low_ref, low_x_ref, low_y_ref, first_ref, 0), (high_ref, high_x_ref, high_y_ref, final_ref, NP - 1)):
            def load(a, i, ref=ref):
                return ref[a, i:i + 8, :]

            def store(a, i, value, out_ref=out_ref):
                out_ref[i:i + 8, :] = value

            tendency(k, (at,), load, lambda a, y, ref=x_ref: ref[0, y:y + 1, :], lambda a, y, ref=y_ref: ref[0, y:y + 1, :], store)
    first, final = first_ref[...], final_ref[...]
    send_a_ref[...] = jnp.where(even, final, first)
    send_b_ref[...] = jnp.where(even, first, final)


def smooth_rows(v, up, down):
    m0, n0 = half_coefs(0.5, 1.0), half_coefs(0.5, 0.0)
    m1, n1 = half_coefs(1.0, 0.5), half_coefs(0.0, 0.5)
    r = [pltpu.roll(piece, 4, axis=0) for piece in v]
    out = []
    for i in range(len(v)):
        if i % 2 == 0:
            other = r[i - 1] if i else up
            out.append(m0 * v[i] if other is None else m0 * v[i] + n0 * other)
        else:
            other = r[i + 1] if i < len(v) - 1 else down
            out.append(m1 * v[i] if other is None else m1 * v[i] + n1 * other)
    return out


def local_kernel(state_hbm, wx_hbm, wy_hbm, adv_hbm, tracer_ref, edge_ref, state, wx, wy, tend, adv, sems, out_sems):
    elements = state.shape[0] // NP
    rows = state.shape[1]
    lower = iota((8, LEV), 0) < 4

    def piece(e):
        return pl.ds(e * NP, NP)

    def copies(e):
        return [pltpu.make_async_copy(src.at[piece(e)], dst.at[piece(e)], sems.at[i, e]) for i, (src, dst) in enumerate(((state_hbm, state), (wx_hbm, wx), (wy_hbm, wy)))]

    def out_copy(e):
        return pltpu.make_async_copy(adv.at[piece(e)], adv_hbm.at[piece(e)], out_sems.at[e])

    for e in range(elements):
        for copy in copies(e):
            copy.start()

    def differentiate(e):
        for copy in copies(e):
            copy.wait()

        def load(a, i):
            return state[e * NP + a, i:i + 8, :]

        def store(a, i, value):
            tend[e * NP + a, i:i + 8, :] = value

        for k in range(rows // 16):
            tendency(k, range(NP), load, lambda a, y: wx[e * NP + a, y:y + 1, :], lambda a, y: wy[e * NP + a, y:y + 1, :], store)

    def finish(e):
        for a in range(NP):
            x = e * NP + a
            v = [tend[x, 8 * i:8 * i + 8, :] for i in range(rows // 8)]
            if a == 0:
                left = jnp.maximum(x - 1, 0)
                share = jnp.where(e > 0, 0.5, 0.0).astype(F32)
                v = [0.5 * v[i] + share * tend[left, 8 * i:8 * i + 8, :] for i in range(rows // 8)]
            if a == NP - 1:
                right = jnp.minimum(x + 1, elements * NP - 1)
                share = jnp.where(e < elements - 1, 0.5, 0.0).astype(F32)
                v = [0.5 * v[i] + share * tend[right, 8 * i:8 * i + 8, :] for i in range(rows // 8)]
            edge_ref[x] = jnp.where(lower, v[0], v[-1])
            for i, value in enumerate(smooth_rows(v, None, None)):
                adv[x, 8 * i:8 * i + 8, :] = state[x, 8 * i:8 * i + 8, :] + value
            tracer_ref[x] = adv[x, pl.ds(1, rows // NT, stride=NT), :]
        out_copy(e).start()

    differentiate(0)

    def step(e, carry):
        differentiate(e)
        finish(e - 1)
        return carry

    lax.fori_loop(1, elements, step, 0)
    finish(elements - 1)
    for e in range(elements):
        out_copy(e).wait()


def edge_kernel(par_ref, edge_ref, got_a_ref, got_b_ref, send_c_ref, send_d_ref):
    even = par_ref[0] == 0
    even_y = par_ref[1] == 0
    px = edge_ref.shape[0]
    rows = got_a_ref.shape[0]
    lower = iota((8, LEV), 0) < 4
    before = jnp.where(even, got_b_ref[...], got_a_ref[...])
    after = jnp.where(even, got_a_ref[...], got_b_ref[...])
    for x in range(px):
        both = edge_ref[x]
        if x == 0:
            both = both + 0.5 * jnp.where(lower, before[0:8], before[rows - 8:rows])
        if x == px - 1:
            both = both + 0.5 * jnp.where(lower, after[0:8], after[rows - 8:rows])
        send_c_ref[x] = jnp.where(even_y, both[4:8], both[0:4])
        send_d_ref[x] = jnp.where(even_y, both[0:4], both[4:8])


def side_shares(even, got_a_ref, got_b_ref, rows):
    before = [0.5 * jnp.where(even, got_b_ref[i:i + 8, :], got_a_ref[i:i + 8, :]) for i in range(0, rows, 8)]
    after = [0.5 * jnp.where(even, got_a_ref[i:i + 8, :], got_b_ref[i:i + 8, :]) for i in range(0, rows, 8)]
    return smooth_rows(before, None, None), smooth_rows(after, None, None)


def rain_kernel(par_ref, cost_ref, bad_ref, tracer_ref, got_a_ref, got_b_ref, got_c_ref, got_d_ref, mask_ref, gain_ref, onehot_ref, first_ref, second_ref, out_ref, rain_ref, side_ref, z_ref):
    px, py, _ = tracer_ref.shape
    half = py // 2
    rows = py * NT
    even_y = par_ref[1] == 0
    for s, side in enumerate(side_shares(par_ref[0] == 0, got_a_ref, got_b_ref, rows)):
        for i, value in enumerate(side):
            side_ref[s, 8 * i:8 * i + 8, :] = value
    at_first = iota((half, LEV), 0) == 0
    at_final = iota((half, LEV), 0) == half - 1

    def advanced(x):
        up = 0.5 * jnp.where(even_y, got_d_ref[x, 1:2, :], got_c_ref[x, 1:2, :])
        down = 0.5 * jnp.where(even_y, got_c_ref[x, 1:2, :], got_d_ref[x, 1:2, :])
        low = tracer_ref[x, 0:half, :] + jnp.where(at_first, up, 0.0)
        high = tracer_ref[x, half:py, :] + jnp.where(at_final, down, 0.0)
        if isinstance(x, int):
            extra = side_ref[0 if x == 0 else 1, pl.ds(1, py, stride=NT), :]
            return low + extra[0:half], high + extra[half:py]
        return low, high

    ones = jnp.ones((2 * LEV, LEV), BF16)
    place = (iota((half, LEV), 1) < 2 * half) & (iota((half, LEV), 1) % half == iota((half, LEV), 0))

    def weigh(x, part, h):
        return part * gain_ref[pl.ds(cost_ref[2 * x + h] - 1, 1), :]

    def step_by_step(x, part, h):
        return part - repeated(part, cost_ref[2 * x + h], first_ref, second_ref)

    def fill(rule):
        def one(x):
            for h, part in enumerate(advanced(x)):
                z_ref[x, half * h:half * h + half, :] = rule(x, part, h)

        one(0)
        one(px - 1)

        def step(x, carry):
            one(x)
            return carry

        lax.fori_loop(1, px - 1, step, 0, unroll=2)

    @pl.when(bad_ref[0] == 0)
    def _():
        fill(weigh)

    @pl.when(bad_ref[0] != 0)
    def _():
        fill(step_by_step)

    def total(x, carry):
        high, low = split2(z_ref[x])
        sums = mm(jnp.concatenate([high, low], axis=1), ones) * 0.125
        for h in range(2):
            spread = jnp.where(place, sums[half * h:half * h + half], 0.0)
            rain_ref[pl.ds(2 * x + h, 1), :] = jnp.sum(spread, axis=0, keepdims=True)
        return carry

    lax.fori_loop(0, px, total, 0, unroll=4)
    lane = iota(out_ref.shape, 1)
    values = jnp.where(lane == 2 * half, 1.0, jnp.where(mask_ref[...] > 0, rain_ref[...], 0.0))
    first = exact_pick(onehot_ref[0], values)
    second = exact_pick(onehot_ref[1], values)
    out_ref[...] = jnp.where(lane < half, first, jnp.where(lane < 2 * half, second, first + second))


def mix_kernel(par_ref, cost_ref, bad_ref, mixing_ref, mask_ref, got_a_ref, got_b_ref, got_c_ref, got_d_ref, first_ref, second_ref, adv_hbm, new_hbm, adv, new, powers, sems, out_sems):
    px, rows, _ = adv.shape
    half = rows // 2
    elements = px // NP
    even_y = par_ref[1] == 0
    lower = iota((8, LEV), 0) < 4

    def piece(e):
        return pl.ds(e * NP, NP)

    def in_copy(e):
        return pltpu.make_async_copy(adv_hbm.at[piece(e)], adv.at[piece(e)], sems.at[e])

    def out_copy(e):
        return pltpu.make_async_copy(new.at[piece(e)], new_hbm.at[piece(e)], out_sems.at[e])

    for e in range(elements):
        in_copy(e).start()

    @pl.when(bad_ref[0] == 0)
    def _():
        powers[0] = jnp.concatenate(split3(mixing_ref[...].T), axis=1)
        for k in (1, 2, 4, 8, 16, 32):
            def part(j):
                return powers[j, :, 0:LEV], powers[j, :, LEV:2 * LEV], powers[j, :, 2 * LEV:3 * LEV]

            first, second = weights(*part(k - 1))

            def step(j, carry):
                powers[j + k] = jnp.concatenate(split3(precise(*part(j), first, second)), axis=1)
                return carry

            lax.fori_loop(0, k, step, 0, unroll=min(k, 4))

    shares = side_shares(par_ref[0] == 0, got_a_ref, got_b_ref, rows)
    for e, x, share in ((0, 0, shares[0]), (elements - 1, px - 1, shares[1])):
        in_copy(e).wait()
        for i in range(rows // 8):
            adv[x, 8 * i:8 * i + 8, :] = adv[x, 8 * i:8 * i + 8, :] + share[i]

    def element(e, carry):
        @pl.when((e > 0) & (e < elements - 1))
        def _():
            in_copy(e).wait()

        rolled = pltpu.roll(mask_ref[...], lax.rem(LEV - e * NP, LEV), axis=1)
        for a in range(NP):
            x = e * NP + a
            up = 0.5 * jnp.where(even_y, got_d_ref[x], got_c_ref[x])
            down = 0.5 * jnp.where(even_y, got_c_ref[x], got_d_ref[x])
            adv[x, 0:4, :] = adv[x, 0:4, :] + up
            adv[x, rows - 4:rows, :] = adv[x, rows - 4:rows, :] + down
            mask = jnp.broadcast_to(rolled[:, a:a + 1], (rows, LEV))

            @pl.when(bad_ref[0] == 0)
            def _():
                for h in range(2):
                    part = slice(half * h, half * h + half)
                    start = adv[x, part, :]
                    high, low = split2(start)
                    both = mm(jnp.concatenate([high, low], axis=0), powers[cost_ref[2 * x + h] - 1, :, 0:2 * LEV])
                    done = (both[:half, :LEV] + both[half:, :LEV]) + (both[:half, LEV:] + both[half:, LEV:])
                    new[x, part, :] = jnp.where(mask[part] > 0.5, done, start)

            @pl.when(bad_ref[0] != 0)
            def _():
                for h in range(2):
                    part = slice(half * h, half * h + half)
                    start = adv[x, part, :]
                    done = repeated(start, cost_ref[2 * x + h], first_ref, second_ref)
                    new[x, part, :] = jnp.where(mask[part] > 0.5, done, start)

        out_copy(e).start()
        return carry

    lax.fori_loop(0, elements, element, 0)
    for e in range(elements):
        out_copy(e).wait()


def gather_kernel(got_ref, rain_ref):
    got = got_ref[...]
    size = got.shape
    half = GROUP_COLS
    count_col = jnp.sum(jnp.where(iota(size, 1) == 2 * half, got, 0.0), axis=1, keepdims=True)
    earlier = jnp.where(iota(size, 0) < iota(size, 1), count_col, 0.0)
    start = jnp.sum(earlier, axis=0, keepdims=True).astype(jnp.int32)
    count = jnp.sum(jnp.where(iota(size, 0) == iota(size, 1), count_col, 0.0), axis=0, keepdims=True).astype(jnp.int32)
    per = LEV // half
    rows = size[0] // per
    slot = (iota(size, 0) % rows) * per + iota(size, 0) // rows
    pick0 = jnp.where((slot == start) & (count > 0), 1.0, 0.0).astype(BF16)
    pick1 = jnp.where((slot == start + 1) & (count > 1), 1.0, 0.0).astype(BF16)
    tile0 = jnp.where(iota(size, 0) == iota(size, 1) % half, 1.0, 0.0).astype(BF16)
    tile1 = jnp.where(iota(size, 0) == iota(size, 1) % half + half, 1.0, 0.0).astype(BF16)

    def tiled(tile):
        high, mid, low = split3(got)
        return mm(high, tile).astype(BF16), mm(mid, tile).astype(BF16), mm(low, tile).astype(BF16)

    total = jnp.zeros(size, F32)
    for pick, tile in ((pick0, tile0), (pick1, tile1)):
        high, mid, low = tiled(tile)
        total = total + ((mm(pick, high) + mm(pick, mid)) + mm(pick, low))
    lane = iota((rows, LEV), 1)
    out = jnp.zeros((rows, LEV), F32)
    for q in range(per):
        out = jnp.where(lane // half == q, total[q * rows:(q + 1) * rows], out)
    rain_ref[...] = out


SMEM = pl.BlockSpec(memory_space=pltpu.SMEM)
VMEM = pl.BlockSpec(memory_space=pltpu.VMEM)
HBM = pl.BlockSpec(memory_space=pltpu.HBM)


def params(mib):
    return pltpu.CompilerParams(vmem_limit_bytes=mib * MIB)


def cost(flops, moved):
    return pl.CostEstimate(flops=flops, bytes_accessed=moved, transcendentals=0)


def body(state, wind_x, wind_y, mixing, triggers, group_costs, destinations):
    px, py, nt, lev = state.shape
    rows = py * nt
    groups = group_costs.shape[0]
    elements = px // NP
    n_elem, n_blk = lax.axis_size("elem"), lax.axis_size("blk")
    slabs = state.reshape(px, rows, lev)
    parity = jnp.stack([lax.axis_index("elem") % 2, lax.axis_index("blk") % 2]).astype(jnp.int32)
    lanes = jnp.pad(jnp.tile(triggers.reshape(groups, GROUP_COLS), (1, 2)), ((0, 0), (0, lev - 2 * GROUP_COLS)))

    def struct(*shape, dtype=F32):
        return jax.ShapeDtypeStruct(shape, dtype)

    def block(shape, *at):
        return pl.BlockSpec(shape, lambda i: at)

    send_a, send_b = pl.pallas_call(
        sides_kernel,
        grid=(1,),
        out_shape=(struct(rows, lev),) * 2,
        in_specs=[
            SMEM,
            block((NP, rows, lev), 0, 0, 0),
            block((NP, rows, lev), elements - 1, 0, 0),
            block((1, py, lev), 0, 0, 0),
            block((1, py, lev), px - 1, 0, 0),
            block((1, py, lev), 0, 0, 0),
            block((1, py, lev), px - 1, 0, 0),
        ],
        out_specs=(block((rows, lev), 0, 0),) * 2,
        scratch_shapes=[pltpu.VMEM((rows, lev), F32)] * 2,
        compiler_params=params(60),
        cost_estimate=cost(2 * MIB, MIB),
        name="sides",
    )(parity, slabs, slabs, wind_x, wind_x, wind_y, wind_y)

    pair_a = [(i, i ^ 1) for i in range(n_elem)]
    pair_b = [(i, (i - 1 if i % 2 == 0 else i + 1) % n_elem) for i in range(n_elem)]
    pair_c = [(j, j ^ 1) for j in range(n_blk)]
    pair_d = [(j, (j - 1 if j % 2 == 0 else j + 1) % n_blk) for j in range(n_blk)]
    got_a = lax.ppermute(send_a, "elem", pair_a)
    got_b = lax.ppermute(send_b, "elem", pair_b)

    local, tracer, edges = pl.pallas_call(
        local_kernel,
        out_shape=(struct(px, rows, lev), struct(px, py, lev), struct(px, 8, lev)),
        in_specs=[HBM, HBM, HBM],
        out_specs=(HBM, VMEM, VMEM),
        scratch_shapes=[
            pltpu.VMEM((px, rows, lev), F32),
            pltpu.VMEM((px, py, lev), F32),
            pltpu.VMEM((px, py, lev), F32),
            pltpu.VMEM((px, rows, lev), F32),
            pltpu.VMEM((px, rows, lev), F32),
            pltpu.SemaphoreType.DMA((3, elements)),
            pltpu.SemaphoreType.DMA((elements,)),
        ],
        compiler_params=params(60),
        cost_estimate=cost(64 * MIB, 12 * MIB),
        name="local",
    )(slabs, wind_x, wind_y)

    send_c, send_d = pl.pallas_call(
        edge_kernel,
        out_shape=(struct(px, nt, lev),) * 2,
        in_specs=[SMEM, VMEM, VMEM, VMEM],
        out_specs=(VMEM, VMEM),
        compiler_params=params(8),
        cost_estimate=cost(MIB, MIB),
        name="edges",
    )(parity, edges, got_a, got_b)
    got_c = lax.ppermute(send_c, "blk", pair_c)
    got_d = lax.ppermute(send_d, "blk", pair_d)

    gains, onehots, mask, first, second, bad = pl.pallas_call(
        gains_kernel,
        out_shape=(
            struct(MAXC, lev),
            struct(2, groups, groups, dtype=BF16),
            struct(rows, lev),
            struct(2 * lev, 2 * lev, dtype=BF16),
            struct(2 * lev, lev, dtype=BF16),
            struct(1, dtype=jnp.int32),
        ),
        in_specs=[VMEM, VMEM, VMEM],
        out_specs=(VMEM, VMEM, VMEM, VMEM, VMEM, SMEM),
        scratch_shapes=[pltpu.VMEM((MAXC, lev), F32)],
        compiler_params=params(8),
        cost_estimate=cost(512 * MIB, MIB),
        name="gains",
    )(mixing, destinations.reshape(1, groups), triggers)

    outgoing = pl.pallas_call(
        rain_kernel,
        out_shape=struct(groups, lev),
        in_specs=[SMEM, SMEM, SMEM] + [VMEM] * 10,
        out_specs=VMEM,
        scratch_shapes=[pltpu.VMEM((groups, lev), F32), pltpu.VMEM((2, rows, lev), F32), pltpu.VMEM((px, py, lev), F32)],
        compiler_params=params(12),
        cost_estimate=cost(64 * MIB, 2 * MIB),
        name="rain",
    )(parity, group_costs, bad, tracer, got_a, got_b, got_c, got_d, lanes, gains, onehots, first, second)

    incoming = lax.all_to_all(outgoing, ("elem", "blk"), split_axis=0, concat_axis=0, tiled=True)

    new = pl.pallas_call(
        mix_kernel,
        out_shape=struct(px, rows, lev),
        in_specs=[SMEM, SMEM, SMEM] + [VMEM] * 8 + [HBM],
        out_specs=HBM,
        scratch_shapes=[
            pltpu.VMEM((px, rows, lev), F32),
            pltpu.VMEM((px, rows, lev), F32),
            pltpu.VMEM((MAXC, lev, 3 * lev), BF16),
            pltpu.SemaphoreType.DMA((elements,)),
            pltpu.SemaphoreType.DMA((elements,)),
        ],
        compiler_params=params(60),
        cost_estimate=cost(4096 * MIB, 10 * MIB),
        name="mix",
    )(parity, group_costs, bad, mixing, mask, got_a, got_b, got_c, got_d, first, second, local)

    rain = pl.pallas_call(
        gather_kernel,
        out_shape=struct(groups * GROUP_COLS // lev, lev),
        in_specs=[VMEM],
        out_specs=VMEM,
        compiler_params=params(8),
        cost_estimate=cost(MIB, MIB),
        name="gather",
    )(incoming)
    return new.reshape(state.shape), rain.reshape(-1)


def solution(mesh):
    return jax.shard_map(
        body,
        mesh=mesh,
        in_specs=(
            P("elem", "blk", None, None),
            P("elem", "blk", None),
            P("elem", "blk", None),
            P(),
            P("elem", "blk"),
            P(("elem", "blk")),
            P(("elem", "blk")),
        ),
        out_specs=(P("elem", "blk", None, None), P(("elem", "blk"))),
        check_vma=False,
    )
```

```python
import functools

import jax
import jax.numpy as jnp
import numpy as np
from jax import lax
from jax.experimental import pallas as pl
from jax.experimental.pallas import tpu as pltpu
from jax.sharding import PartitionSpec as P

NP = 4
NT = 4
LEV = 128
GROUP_COLS = 16
MAXC = 64
LIMIT = 1.0e3
F32 = jnp.float32
BF16 = jnp.bfloat16
MIB = 1024 * 1024


def gll_derivative():
    nodes = np.array([-1.0, -1.0 / np.sqrt(5.0), 1.0 / np.sqrt(5.0), 1.0])
    legendre = (5.0 * nodes * nodes * nodes - 3.0 * nodes) / 2.0
    derivative = np.zeros((4, 4))
    for a in range(4):
        for b in range(4):
            if a != b:
                derivative[a, b] = legendre[a] / (legendre[b] * (nodes[a] - nodes[b]))
    derivative[0, 0] = -3.0
    derivative[3, 3] = 3.0
    return derivative


def split2(x):
    high = x.astype(BF16)
    return high, (x - high.astype(F32)).astype(BF16)


def split3(x):
    high = x.astype(BF16)
    rest = x - high.astype(F32)
    mid = rest.astype(BF16)
    return high, mid, (rest - mid.astype(F32)).astype(BF16)


def mm(a, b):
    return jnp.dot(a, b, preferred_element_type=F32)


def exact_pick(onehot, values):
    high, mid, low = split3(values)
    return mm(onehot, high) + mm(onehot, mid) + mm(onehot, low)


def weights(high, mid, low):
    pair = jnp.concatenate([high, mid], axis=1)
    return jnp.concatenate([pair, pair], axis=0), jnp.concatenate([low, high], axis=0)


def precise(high, mid, low, first, second):
    one = mm(jnp.concatenate([high, mid], axis=1), first)
    two = mm(jnp.concatenate([high, low], axis=1), second)
    return one[:, :LEV] + (one[:, LEV:] + two)


def repeated(start, cost, first_ref, second_ref):
    return lax.fori_loop(0, cost, lambda i, c: precise(*split3(c), first_ref[...], second_ref[...]), start)


def iota(shape, dim):
    return lax.broadcasted_iota(jnp.int32, shape, dim)


def gains_kernel(mixing_ref, dest_ref, trig_ref, gain_ref, onehot_ref, lanes_ref, first_ref, second_ref, bad_ref, sums):
    square = mixing_ref[...]
    worst = jnp.max(jnp.abs(square))
    first_ref[...], second_ref[...] = weights(*split3(square.T))
    sums[0:8] = jnp.broadcast_to(jnp.sum(square, axis=0, keepdims=True), (8, LEV))
    for k in (1, 2, 4, 8, 16, 32):
        parts = split3(square)
        pair = weights(*parts)
        rows = max(k, 8)
        grown = precise(*split3(sums[0:rows]), *pair)
        if k < 8:
            pick = iota((8, LEV), 0)
            merged = sums[0:8]
            for j in range(k):
                merged = jnp.where(pick == j + k, grown[j:j + 1], merged)
            sums[0:8] = merged
        else:
            sums[k:2 * k] = grown
        if k < 32:
            square = precise(*parts, *pair)
            worst = jnp.maximum(worst, jnp.max(jnp.abs(square)))
    gain_ref[...] = 1.0 - sums[...]
    bad_ref[0] = jnp.where(worst <= LIMIT, 0, 1).astype(jnp.int32)

    groups = dest_ref.shape[1]
    shape = (groups, groups)
    dest_row = jnp.broadcast_to(dest_ref[...], shape)
    diagonal = iota(shape, 0) == iota(shape, 1)
    dest_col = jnp.sum(jnp.where(diagonal, dest_row, 0), axis=1, keepdims=True)
    earlier = (dest_col == dest_row) & (iota(shape, 0) < iota(shape, 1))
    within = jnp.sum(jnp.where(earlier, 1, 0), axis=0, keepdims=True)
    at = dest_row == iota(shape, 0)
    onehot_ref[0] = jnp.where(at & (within == 0), 1.0, 0.0).astype(BF16)
    onehot_ref[1] = jnp.where(at & (within == 1), 1.0, 0.0).astype(BF16)

    px, py = trig_ref.shape
    half = py // 2
    wide = trig_ref[...].astype(F32).astype(BF16)
    table = jnp.zeros((groups, LEV), F32)
    for h in range(2):
        chosen = jnp.where(iota((groups, px), 0) == 2 * iota((groups, px), 1) + h, 1.0, 0.0).astype(BF16)
        lane = iota((py, LEV), 1)
        placed = jnp.where((lane < 2 * half) & (lane % half + half * h == iota((py, LEV), 0)), 1.0, 0.0).astype(BF16)
        table = table + mm(mm(chosen, wide).astype(BF16), placed)
    lanes_ref[...] = table


def half_coefs(first, second):
    return jnp.where(iota((8, LEV), 0) < 4, F32(first), F32(second))


def derivative_tables():
    deriv = -0.05 * gll_derivative()
    g = [[float(np.float32(deriv[a, b])) for b in range(4)] for a in range(4)]
    low = [half_coefs(g[0][0], g[1][1]), half_coefs(g[0][1], g[1][0]), half_coefs(g[0][2], g[1][3]), half_coefs(g[0][3], g[1][2])]
    high = [half_coefs(g[2][0], g[3][1]), half_coefs(g[2][1], g[3][0]), half_coefs(g[2][2], g[3][3]), half_coefs(g[2][3], g[3][2])]
    return g, low, high


def tendency(k, points, load, load_x, load_y, store):
    g, low, high = derivative_tables()
    lower = iota((8, LEV), 0) < 4
    v = [[load(a, 16 * k + 8 * h) for h in range(2)] for a in range(NP)]
    for a in points:
        r = [pltpu.roll(v[a][h], 4, axis=0) for h in range(2)]
        for h, coefs in ((0, low), (1, high)):
            along_y = (coefs[0] * v[a][0] + coefs[1] * r[0]) + (coefs[2] * v[a][1] + coefs[3] * r[1])
            along_x = (g[a][0] * v[0][h] + g[a][1] * v[1][h]) + (g[a][2] * v[2][h] + g[a][3] * v[3][h])
            y = 4 * k + 2 * h
            wx = jnp.where(lower, load_x(a, y), load_x(a, y + 1))
            wy = jnp.where(lower, load_y(a, y), load_y(a, y + 1))
            store(a, 16 * k + 8 * h, wx * along_x + wy * along_y)


def sides_kernel(state_hbm, wx_hbm, wy_hbm, send_a_ref, send_b_ref, state, wx, wy, ends, sems):
    even = lax.axis_index("elem") % 2 == 0
    px = state_hbm.shape[0]
    copies = []
    for i, (element, x) in enumerate(((0, 0), (px - NP, px - 1))):
        copies.append(pltpu.make_async_copy(state_hbm.at[pl.ds(element, NP)], state.at[i], sems.at[i]))
        copies.append(pltpu.make_async_copy(wx_hbm.at[x], wx.at[i], sems.at[2 + i]))
        copies.append(pltpu.make_async_copy(wy_hbm.at[x], wy.at[i], sems.at[4 + i]))
    for copy in copies:
        copy.start()
    for copy in copies:
        copy.wait()
    for k in range(state.shape[2] // 16):
        for s, at in ((0, 0), (1, NP - 1)):
            def load(a, i):
                return state[s, a, i:i + 8, :]

            def store(a, i, value):
                ends[s, i:i + 8, :] = value

            tendency(k, (at,), load, lambda a, y: wx[s, y:y + 1, :], lambda a, y: wy[s, y:y + 1, :], store)
    send_a_ref[...] = jnp.where(even, ends[1], ends[0])
    send_b_ref[...] = jnp.where(even, ends[0], ends[1])


def smooth_rows(v, up, down):
    m0, n0 = half_coefs(0.5, 1.0), half_coefs(0.5, 0.0)
    m1, n1 = half_coefs(1.0, 0.5), half_coefs(0.0, 0.5)
    r = [pltpu.roll(piece, 4, axis=0) for piece in v]
    out = []
    for i in range(len(v)):
        if i % 2 == 0:
            other = r[i - 1] if i else up
            out.append(m0 * v[i] if other is None else m0 * v[i] + n0 * other)
        else:
            other = r[i + 1] if i < len(v) - 1 else down
            out.append(m1 * v[i] if other is None else m1 * v[i] + n1 * other)
    return out


def local_kernel(state, wx, wy, adv_hbm, tracer_ref, edge_ref, tend, adv, sems):
    elements = state.shape[0] // NP
    rows = state.shape[1]
    lower = iota((8, LEV), 0) < 4

    def out_copy(e):
        piece = pl.ds(e * NP, NP)
        return pltpu.make_async_copy(adv.at[piece], adv_hbm.at[piece], sems.at[e])

    def differentiate(e):
        def load(a, i):
            return state[e * NP + a, i:i + 8, :]

        def store(a, i, value):
            tend[e * NP + a, i:i + 8, :] = value

        for k in range(rows // 16):
            tendency(k, range(NP), load, lambda a, y: wx[e * NP + a, y:y + 1, :], lambda a, y: wy[e * NP + a, y:y + 1, :], store)

    def finish(e):
        for a in range(NP):
            x = e * NP + a
            v = [tend[x, 8 * i:8 * i + 8, :] for i in range(rows // 8)]
            if a == 0:
                left = jnp.maximum(x - 1, 0)
                share = jnp.where(e > 0, 0.5, 0.0).astype(F32)
                v = [0.5 * v[i] + share * tend[left, 8 * i:8 * i + 8, :] for i in range(rows // 8)]
            if a == NP - 1:
                right = jnp.minimum(x + 1, elements * NP - 1)
                share = jnp.where(e < elements - 1, 0.5, 0.0).astype(F32)
                v = [0.5 * v[i] + share * tend[right, 8 * i:8 * i + 8, :] for i in range(rows // 8)]
            edge_ref[x] = jnp.where(lower, v[0], v[-1])
            for i, value in enumerate(smooth_rows(v, None, None)):
                adv[x, 8 * i:8 * i + 8, :] = state[x, 8 * i:8 * i + 8, :] + value
            tracer_ref[x] = adv[x, pl.ds(1, rows // NT, stride=NT), :]
        out_copy(e).start()

    differentiate(0)

    def step(e, carry):
        differentiate(e)
        finish(e - 1)
        return carry

    lax.fori_loop(1, elements, step, 0)
    finish(elements - 1)
    for e in range(elements):
        out_copy(e).wait()


def edge_kernel(edge_ref, got_a_ref, got_b_ref, send_c_ref, send_d_ref):
    even = lax.axis_index("elem") % 2 == 0
    even_y = lax.axis_index("blk") % 2 == 0
    px = edge_ref.shape[0]
    rows = got_a_ref.shape[0]
    lower = iota((8, LEV), 0) < 4
    before = jnp.where(even, got_b_ref[...], got_a_ref[...])
    after = jnp.where(even, got_a_ref[...], got_b_ref[...])
    for x in range(px):
        both = edge_ref[x]
        if x == 0:
            both = both + 0.5 * jnp.where(lower, before[0:8], before[rows - 8:rows])
        if x == px - 1:
            both = both + 0.5 * jnp.where(lower, after[0:8], after[rows - 8:rows])
        send_c_ref[x] = jnp.where(even_y, both[4:8], both[0:4])
        send_d_ref[x] = jnp.where(even_y, both[0:4], both[4:8])


def side_shares(even, got_a_ref, got_b_ref, rows):
    before = [0.5 * jnp.where(even, got_b_ref[i:i + 8, :], got_a_ref[i:i + 8, :]) for i in range(0, rows, 8)]
    after = [0.5 * jnp.where(even, got_a_ref[i:i + 8, :], got_b_ref[i:i + 8, :]) for i in range(0, rows, 8)]
    return smooth_rows(before, None, None), smooth_rows(after, None, None)


def rain_kernel(cost_ref, bad_ref, tracer_ref, got_a_ref, got_b_ref, got_c_ref, got_d_ref, mask_ref, gain_ref, onehot_ref, first_ref, second_ref, out_ref, rain_ref, side_ref):
    px, py, _ = tracer_ref.shape
    half = py // 2
    rows = py * NT
    even_y = lax.axis_index("blk") % 2 == 0
    for s, side in enumerate(side_shares(lax.axis_index("elem") % 2 == 0, got_a_ref, got_b_ref, rows)):
        for i, value in enumerate(side):
            side_ref[s, 8 * i:8 * i + 8, :] = value
    at_first = iota((half, LEV), 0) == 0
    at_final = iota((half, LEV), 0) == half - 1

    def advanced(x):
        up = 0.5 * jnp.where(even_y, got_d_ref[x, 1:2, :], got_c_ref[x, 1:2, :])
        down = 0.5 * jnp.where(even_y, got_c_ref[x, 1:2, :], got_d_ref[x, 1:2, :])
        low = tracer_ref[x, 0:half, :] + jnp.where(at_first, up, 0.0)
        high = tracer_ref[x, half:py, :] + jnp.where(at_final, down, 0.0)
        if isinstance(x, int):
            extra = side_ref[0 if x == 0 else 1, pl.ds(1, py, stride=NT), :]
            return low + extra[0:half], high + extra[half:py]
        return low, high

    place = (iota((half, LEV), 1) < 2 * half) & (iota((half, LEV), 1) % half == iota((half, LEV), 0))

    def weigh(x, part, h):
        return part * gain_ref[pl.ds(cost_ref[2 * x + h] - 1, 1), :]

    def step_by_step(x, part, h):
        return part - repeated(part, cost_ref[2 * x + h], first_ref, second_ref)

    def fill(rule, unroll):
        def one(x):
            for h, part in enumerate(advanced(x)):
                sums = jnp.sum(rule(x, part, h), axis=1, keepdims=True) * 0.125
                rain_ref[pl.ds(2 * x + h, 1), :] = jnp.sum(jnp.where(place, sums, 0.0), axis=0, keepdims=True)

        one(0)
        one(px - 1)

        def step(x, carry):
            one(x)
            return carry

        lax.fori_loop(1, px - 1, step, 0, unroll=unroll)

    @pl.when(bad_ref[0] == 0)
    def _():
        fill(weigh, 31)

    @pl.when(bad_ref[0] != 0)
    def _():
        fill(step_by_step, 1)

    lane = iota(out_ref.shape, 1)
    values = jnp.where(lane == 2 * half, 1.0, jnp.where(mask_ref[...] > 0.5, rain_ref[...], 0.0))
    first = exact_pick(onehot_ref[0], values)
    second = exact_pick(onehot_ref[1], values)
    out_ref[...] = jnp.where(lane < half, first, jnp.where(lane < 2 * half, second, first + second))


def mix_kernel(cost_ref, bad_ref, mixing_hbm, trig_hbm, got_a_hbm, got_b_hbm, got_c_hbm, got_d_hbm, first_hbm, second_hbm, adv_hbm, new_hbm, adv, new, powers, mixing_ref, trig_ref, got_a_ref, got_b_ref, got_c_ref, got_d_ref, first_ref, second_ref, mask_ref, sems, out_sems, small_sems):
    px, rows, _ = adv.shape
    py = rows // NT
    half = rows // 2
    chunks = sems.shape[0]
    size = px // chunks
    even_y = lax.axis_index("blk") % 2 == 0
    lower = iota((8, LEV), 0) < 4

    def in_copy(i):
        return pltpu.make_async_copy(adv_hbm.at[pl.ds(i * size, size)], adv.at[pl.ds(i * size, size)], sems.at[i])

    def out_copy(i):
        return pltpu.make_async_copy(new.at[pl.ds(i * size, size)], new_hbm.at[pl.ds(i * size, size)], out_sems.at[i])

    small = [
        pltpu.make_async_copy(src, dst, small_sems.at[i])
        for i, (src, dst) in enumerate(
            (
                (mixing_hbm, mixing_ref),
                (trig_hbm, trig_ref),
                (got_a_hbm, got_a_ref),
                (got_b_hbm, got_b_ref),
                (got_c_hbm, got_c_ref),
                (got_d_hbm, got_d_ref),
                (first_hbm, first_ref),
                (second_hbm, second_ref),
            )
        )
    ]
    for copy in small:
        copy.start()
    for i in range(chunks):
        in_copy(i).start()
    small[0].wait()

    @pl.when(bad_ref[0] == 0)
    def _():
        powers[0] = jnp.concatenate(split3(mixing_ref[...].T), axis=1)

        def part(j):
            return powers[j, :, 0:LEV], powers[j, :, LEV:2 * LEV], powers[j, :, 2 * LEV:3 * LEV]

        for k in (1, 2, 4, 8):
            first, second = weights(*part(k - 1))

            def step(j, carry):
                powers[j + k] = jnp.concatenate(split3(precise(*part(j), first, second)), axis=1)
                return carry

            lax.fori_loop(0, k, step, 0, unroll=True)

        for k in (16, 32):
            pair = powers[k - 1, :, 0:2 * LEV]
            both = jnp.concatenate([pair, pair], axis=0)

            def later(j, carry):
                value = mm(powers[j, :, 0:2 * LEV], both)
                powers[j + k, :, 0:2 * LEV] = jnp.concatenate(split2(value[:, :LEV] + value[:, LEV:]), axis=1)
                return carry

            lax.fori_loop(0, k, later, 0, unroll=8)

    for copy in small[1:]:
        copy.wait()
    trig = jnp.concatenate([trig_ref[...].astype(F32), jnp.zeros((LEV - px, py), F32)], axis=0).T
    spread = jnp.where(iota((rows, py), 0) // NT == iota((rows, py), 1), 1.0, 0.0).astype(BF16)
    mask_ref[...] = mm(spread, trig.astype(BF16))
    shares = side_shares(lax.axis_index("elem") % 2 == 0, got_a_ref, got_b_ref, rows)
    in_copy(0).wait()
    in_copy(chunks - 1).wait()
    for x, share in ((0, shares[0]), (px - 1, shares[1])):
        for i in range(rows // 8):
            adv[x, 8 * i:8 * i + 8, :] = adv[x, 8 * i:8 * i + 8, :] + share[i]

    def edged(x, h):
        start = adv[x, half * h:half * h + half, :]
        if h == 0:
            add = 0.5 * jnp.where(even_y, got_d_ref[x], got_c_ref[x])
            return jnp.concatenate([start[0:8] + jnp.where(lower, jnp.concatenate([add, add], axis=0), 0.0), start[8:]], axis=0)
        add = 0.5 * jnp.where(even_y, got_c_ref[x], got_d_ref[x])
        return jnp.concatenate([start[:half - 8], start[half - 8:] + jnp.where(lower, 0.0, jnp.concatenate([add, add], axis=0))], axis=0)

    def powered(x, h, start):
        high, low = split2(start)
        both = mm(jnp.concatenate([high, low], axis=0), powers[cost_ref[2 * x + h] - 1, :, 0:2 * LEV])
        return (both[:half, :LEV] + both[half:, :LEV]) + (both[:half, LEV:] + both[half:, LEV:])

    def step_by_step(x, h, start):
        return repeated(start, cost_ref[2 * x + h], first_ref, second_ref)

    def one(rule, x, mask):
        for h in range(2):
            start = edged(x, h)
            done = rule(x, h, start)
            new[x, half * h:half * h + half, :] = jnp.where(mask[half * h:half * h + half] > 0.5, done, start)

    def arrive(i):
        @pl.when((i > 0) & (i < chunks - 1))
        def _():
            in_copy(i).wait()

    @pl.when(bad_ref[0] == 0)
    def _():
        def chunk(i, carry):
            arrive(i)
            rolled = pltpu.roll(mask_ref[...], lax.rem(LEV - i * size, LEV), axis=1)
            for a in range(size):
                one(powered, i * size + a, jnp.broadcast_to(rolled[:, a:a + 1], (rows, LEV)))
            out_copy(i).start()
            return carry

        lax.fori_loop(0, chunks, chunk, 0)

    @pl.when(bad_ref[0] != 0)
    def _():
        def chunk(i, carry):
            arrive(i)

            def column(a, carry):
                x = i * size + a
                rolled = pltpu.roll(mask_ref[...], lax.rem(LEV - x, LEV), axis=1)
                one(step_by_step, x, jnp.broadcast_to(rolled[:, 0:1], (rows, LEV)))
                return carry

            lax.fori_loop(0, size, column, 0)
            out_copy(i).start()
            return carry

        lax.fori_loop(0, chunks, chunk, 0)

    for i in range(chunks):
        out_copy(i).wait()


def gather_kernel(got_ref, rain_ref):
    got = got_ref[...]
    size = got.shape
    half = GROUP_COLS
    count_col = jnp.sum(jnp.where(iota(size, 1) == 2 * half, got, 0.0), axis=1, keepdims=True)
    earlier = jnp.where(iota(size, 0) < iota(size, 1), count_col, 0.0)
    start = jnp.sum(earlier, axis=0, keepdims=True).astype(jnp.int32)
    count = jnp.sum(jnp.where(iota(size, 0) == iota(size, 1), count_col, 0.0), axis=0, keepdims=True).astype(jnp.int32)
    per = LEV // half
    rows = size[0] // per
    slot = (iota(size, 0) % rows) * per + iota(size, 0) // rows
    pick0 = jnp.where((slot == start) & (count > 0), 1.0, 0.0).astype(BF16)
    pick1 = jnp.where((slot == start + 1) & (count > 1), 1.0, 0.0).astype(BF16)
    tile0 = jnp.where(iota(size, 0) == iota(size, 1) % half, 1.0, 0.0).astype(BF16)
    tile1 = jnp.where(iota(size, 0) == iota(size, 1) % half + half, 1.0, 0.0).astype(BF16)

    def tiled(tile):
        high, mid, low = split3(got)
        return mm(high, tile).astype(BF16), mm(mid, tile).astype(BF16), mm(low, tile).astype(BF16)

    total = jnp.zeros(size, F32)
    for pick, tile in ((pick0, tile0), (pick1, tile1)):
        high, mid, low = tiled(tile)
        total = total + ((mm(pick, high) + mm(pick, mid)) + mm(pick, low))
    lane = iota((rows, LEV), 1)
    out = jnp.zeros((rows, LEV), F32)
    for q in range(per):
        out = jnp.where(lane // half == q, total[q * rows:(q + 1) * rows], out)
    rain_ref[...] = out


SMEM = pl.BlockSpec(memory_space=pltpu.SMEM)
VMEM = pl.BlockSpec(memory_space=pltpu.VMEM)
HBM = pl.BlockSpec(memory_space=pltpu.HBM)


def params(mib):
    return pltpu.CompilerParams(vmem_limit_bytes=mib * MIB)


def cost(flops, moved):
    return pl.CostEstimate(flops=flops, bytes_accessed=moved, transcendentals=0)


def body(state, wind_x, wind_y, mixing, triggers, group_costs, destinations):
    px, py, nt, lev = state.shape
    rows = py * nt
    groups = group_costs.shape[0]
    elements = px // NP
    n_elem, n_blk = lax.axis_size("elem"), lax.axis_size("blk")
    slabs = state.reshape(px, rows, lev)
    def struct(*shape, dtype=F32):
        return jax.ShapeDtypeStruct(shape, dtype)

    def block(shape, *at):
        return pl.BlockSpec(shape, lambda i: at)

    def kept(x):
        return pltpu.with_memory_space_constraint(x, pltpu.HBM)

    send_a, send_b = pl.pallas_call(
        sides_kernel,
        out_shape=(struct(rows, lev),) * 2,
        in_specs=[HBM] * 3,
        out_specs=(VMEM, VMEM),
        scratch_shapes=[
            pltpu.VMEM((2, NP, rows, lev), F32),
            pltpu.VMEM((2, py, lev), F32),
            pltpu.VMEM((2, py, lev), F32),
            pltpu.VMEM((2, rows, lev), F32),
            pltpu.SemaphoreType.DMA((6,)),
        ],
        compiler_params=params(4),
        cost_estimate=cost(2 * MIB, MIB),
        name="sides",
    )(kept(slabs), kept(wind_x), kept(wind_y))

    pair_a = [(i, i ^ 1) for i in range(n_elem)]
    pair_b = [(i, (i - 1 if i % 2 == 0 else i + 1) % n_elem) for i in range(n_elem)]
    pair_c = [(j, j ^ 1) for j in range(n_blk)]
    pair_d = [(j, (j - 1 if j % 2 == 0 else j + 1) % n_blk) for j in range(n_blk)]
    got_a = lax.ppermute(send_a, "elem", pair_a)
    got_b = lax.ppermute(send_b, "elem", pair_b)

    local, tracer, edges = pl.pallas_call(
        local_kernel,
        out_shape=(pltpu.HBM((px, rows, lev), F32), struct(px, py, lev), struct(px, 8, lev)),
        in_specs=[VMEM, VMEM, VMEM],
        out_specs=(HBM, VMEM, VMEM),
        scratch_shapes=[
            pltpu.VMEM((px, rows, lev), F32),
            pltpu.VMEM((px, rows, lev), F32),
            pltpu.SemaphoreType.DMA((elements,)),
        ],
        compiler_params=params(14),
        cost_estimate=cost(64 * MIB, 12 * MIB),
        name="local",
    )(slabs, wind_x, wind_y)

    send_c, send_d = pl.pallas_call(
        edge_kernel,
        out_shape=(struct(px, nt, lev),) * 2,
        in_specs=[VMEM, VMEM, VMEM],
        out_specs=(VMEM, VMEM),
        compiler_params=params(8),
        cost_estimate=cost(MIB, MIB),
        name="edges",
    )(edges, got_a, got_b)
    got_c = lax.ppermute(send_c, "blk", pair_c)
    got_d = lax.ppermute(send_d, "blk", pair_d)

    gains, onehots, lanes, first, second, bad = pl.pallas_call(
        gains_kernel,
        out_shape=(
            struct(MAXC, lev),
            struct(2, groups, groups, dtype=BF16),
            struct(groups, lev),
            struct(2 * lev, 2 * lev, dtype=BF16),
            struct(2 * lev, lev, dtype=BF16),
            struct(1, dtype=jnp.int32),
        ),
        in_specs=[VMEM, VMEM, VMEM],
        out_specs=(VMEM, VMEM, VMEM, VMEM, VMEM, SMEM),
        scratch_shapes=[pltpu.VMEM((MAXC, lev), F32)],
        compiler_params=params(8),
        cost_estimate=cost(512 * MIB, MIB),
        name="gains",
    )(mixing, destinations.reshape(1, groups), triggers)

    outgoing = pl.pallas_call(
        rain_kernel,
        out_shape=struct(groups, lev),
        in_specs=[SMEM, SMEM] + [VMEM] * 10,
        out_specs=VMEM,
        scratch_shapes=[pltpu.VMEM((groups, lev), F32), pltpu.VMEM((2, rows, lev), F32)],
        compiler_params=params(12),
        cost_estimate=cost(64 * MIB, 2 * MIB),
        name="rain",
    )(group_costs, bad, tracer, got_a, got_b, got_c, got_d, lanes, gains, onehots, first, second)

    incoming = lax.all_to_all(outgoing, ("elem", "blk"), split_axis=0, concat_axis=0, tiled=True)

    chunks = 4
    new = pl.pallas_call(
        mix_kernel,
        out_shape=struct(px, rows, lev),
        in_specs=[SMEM, SMEM] + [HBM] * 9,
        out_specs=HBM,
        scratch_shapes=[
            pltpu.VMEM((px, rows, lev), F32),
            pltpu.VMEM((px, rows, lev), F32),
            pltpu.VMEM((MAXC, lev, 3 * lev), BF16),
            pltpu.VMEM((lev, lev), F32),
            pltpu.VMEM((px, py), jnp.int32),
            pltpu.VMEM((rows, lev), F32),
            pltpu.VMEM((rows, lev), F32),
            pltpu.VMEM((px, nt, lev), F32),
            pltpu.VMEM((px, nt, lev), F32),
            pltpu.VMEM((2 * lev, 2 * lev), BF16),
            pltpu.VMEM((2 * lev, lev), BF16),
            pltpu.VMEM((rows, lev), F32),
            pltpu.SemaphoreType.DMA((chunks,)),
            pltpu.SemaphoreType.DMA((chunks,)),
            pltpu.SemaphoreType.DMA((8,)),
        ],
        compiler_params=params(60),
        cost_estimate=cost(4096 * MIB, 10 * MIB),
        name="mix",
    )(group_costs, bad, mixing, triggers, got_a, got_b, got_c, got_d, first, second, kept(local))

    rain = pl.pallas_call(
        gather_kernel,
        out_shape=struct(groups * GROUP_COLS // lev, lev),
        in_specs=[VMEM],
        out_specs=VMEM,
        compiler_params=params(8),
        cost_estimate=cost(MIB, MIB),
        name="gather",
    )(incoming)
    return new.reshape(state.shape), rain.reshape(-1)


def solution(mesh):
    return jax.shard_map(
        body,
        mesh=mesh,
        in_specs=(
            P("elem", "blk", None, None),
            P("elem", "blk", None),
            P("elem", "blk", None),
            P(),
            P("elem", "blk"),
            P(("elem", "blk")),
            P(("elem", "blk")),
        ),
        out_specs=(P("elem", "blk", None, None), P(("elem", "blk"))),
        check_vma=False,
    )
```

```python
import functools

import jax
import jax.numpy as jnp
import numpy as np
from jax import lax
from jax.experimental import pallas as pl
from jax.experimental.pallas import tpu as pltpu
from jax.sharding import PartitionSpec as P

NP = 4
NT = 4
LEV = 128
GROUP_COLS = 16
MAXC = 64
LIMIT = 1.0e3
F32 = jnp.float32
BF16 = jnp.bfloat16
MIB = 1024 * 1024


def gll_derivative():
    nodes = np.array([-1.0, -1.0 / np.sqrt(5.0), 1.0 / np.sqrt(5.0), 1.0])
    legendre = (5.0 * nodes * nodes * nodes - 3.0 * nodes) / 2.0
    derivative = np.zeros((4, 4))
    for a in range(4):
        for b in range(4):
            if a != b:
                derivative[a, b] = legendre[a] / (legendre[b] * (nodes[a] - nodes[b]))
    derivative[0, 0] = -3.0
    derivative[3, 3] = 3.0
    return derivative


def split2(x):
    high = x.astype(BF16)
    return high, (x - high.astype(F32)).astype(BF16)


def split3(x):
    high = x.astype(BF16)
    rest = x - high.astype(F32)
    mid = rest.astype(BF16)
    return high, mid, (rest - mid.astype(F32)).astype(BF16)


def mm(a, b):
    return jnp.dot(a, b, preferred_element_type=F32)


def exact_pick(onehot, values):
    return mm(jnp.concatenate([onehot] * 3, axis=1), jnp.concatenate(split3(values), axis=0))


def weights(high, mid, low):
    pair = jnp.concatenate([high, mid], axis=1)
    return jnp.concatenate([pair, pair], axis=0), jnp.concatenate([low, high], axis=0)


def precise(high, mid, low, first, second):
    one = mm(jnp.concatenate([high, mid], axis=1), first)
    two = mm(jnp.concatenate([high, low], axis=1), second)
    return one[:, :LEV] + (one[:, LEV:] + two)


def repeated(start, cost, first_ref, second_ref):
    return lax.fori_loop(0, cost, lambda i, c: precise(*split3(c), first_ref[...], second_ref[...]), start)


def iota(shape, dim):
    return lax.broadcasted_iota(jnp.int32, shape, dim)


def gains_kernel(mixing_ref, dest_ref, cost_ref, trig_ref, table_ref, onehot_ref, lanes_ref, costs_ref, first_ref, second_ref, bad_ref, sums):
    square = mixing_ref[...]
    worst = jnp.max(jnp.abs(square))
    first_ref[...], second_ref[...] = weights(*split3(square.T))
    sums[0:8] = jnp.broadcast_to(jnp.sum(square, axis=0, keepdims=True), (8, LEV))
    for k in (1, 2, 4, 8, 16, 32):
        parts = split3(square)
        pair = weights(*parts)
        rows = max(k, 8)
        grown = precise(*split3(sums[0:rows]), *pair)
        if k < 8:
            pick = iota((8, LEV), 0)
            merged = sums[0:8]
            for j in range(k):
                merged = jnp.where(pick == j + k, grown[j:j + 1], merged)
            sums[0:8] = merged
        else:
            sums[k:2 * k] = grown
        if k < 32:
            square = precise(*parts, *pair)
            worst = jnp.maximum(worst, jnp.max(jnp.abs(square)))
    bad_ref[...] = jnp.full(bad_ref.shape, jnp.where(worst <= LIMIT, 0.0, 1.0), F32)

    px, py = trig_ref.shape
    half = py // 2
    groups = 2 * px
    shape = (groups, groups)
    first_at, second_at = iota(shape, 0), iota(shape, 1)
    number0 = 2 * (first_at % px) + first_at // px
    number1 = 2 * (second_at % px) + second_at // px
    diagonal = first_at == number1

    def across(row):
        return jnp.sum(jnp.where(first_at == second_at, row, 0), axis=1, keepdims=True)

    def ordered(row_ref):
        col = across(jnp.broadcast_to(row_ref[...], shape))
        return jnp.sum(jnp.where(diagonal, col, 0), axis=0, keepdims=True)

    dest_row = jnp.broadcast_to(ordered(dest_ref), shape)
    dest_col = across(dest_row)
    earlier = (dest_col == dest_row) & (number0 < number1)
    within = jnp.sum(jnp.where(earlier, 1, 0), axis=0, keepdims=True)
    at = dest_row == first_at
    onehot_ref[0:groups] = jnp.where(at & (within == 0), 1.0, 0.0).astype(BF16)
    onehot_ref[groups:2 * groups] = jnp.where(at & (within == 1), 1.0, 0.0).astype(BF16)

    cost_col = across(jnp.broadcast_to(ordered(cost_ref), shape))
    chosen = jnp.where(cost_col == iota((groups, MAXC), 1) + 1, 1.0, 0.0).astype(BF16)
    table_ref[...] = exact_pick(chosen, 1.0 - sums[...])
    costs_ref[...] = jnp.broadcast_to(cost_col, (groups, LEV)).astype(F32)

    wide = trig_ref[...].astype(F32).astype(BF16)
    lane = iota((py, LEV), 1)
    for h in range(2):
        placed = jnp.where((lane < 2 * half) & (lane % half + half * h == iota((py, LEV), 0)), 1.0, 0.0).astype(BF16)
        lanes_ref[h * px:h * px + px] = mm(wide, placed)


def half_coefs(first, second):
    return jnp.where(iota((8, LEV), 0) < 4, F32(first), F32(second))


def derivative_tables():
    deriv = -0.05 * gll_derivative()
    even = [float(np.float32(0.5 * (deriv[a, 0] + deriv[a, 3]))) for a in range(2)]
    odd = [[float(np.float32(0.5 * (deriv[a, b] - deriv[a, 3 - b]))) for b in range(2)] for a in range(2)]
    return even, odd


def tendency(k, points, load, load_x, load_y, store):
    even, odd = derivative_tables()
    c_even = half_coefs(even[0], -even[1])
    c_odd, c_cross = half_coefs(odd[0][0], odd[1][1]), half_coefs(odd[0][1], odd[1][0])
    lower = iota((8, LEV), 0) < 4
    v = [[load(a, 16 * k + 8 * h) for h in range(2)] for a in range(NP)]
    along_x = []
    for h in range(2):
        d0, d1 = v[0][h] - v[3][h], v[1][h] - v[2][h]
        mean = (v[0][h] + v[3][h]) - (v[1][h] + v[2][h])
        p0, p1 = even[0] * mean, even[1] * mean
        q0, q1 = odd[0][0] * d0 + odd[0][1] * d1, odd[1][0] * d0 + odd[1][1] * d1
        along_x.append((q0 + p0, q1 + p1, q1 - p1, q0 - p0))
    for a in points:
        r1 = pltpu.roll(v[a][1], 4, axis=0)
        add, sub = v[a][0] + r1, v[a][0] - r1
        odds = c_odd * sub + c_cross * pltpu.roll(sub, 4, axis=0)
        evens = c_even * (add - pltpu.roll(add, 4, axis=0))
        along_y = (odds + evens, pltpu.roll(odds - evens, 4, axis=0))
        for h in range(2):
            y = 4 * k + 2 * h
            wx = jnp.where(lower, load_x(a, y), load_x(a, y + 1))
            wy = jnp.where(lower, load_y(a, y), load_y(a, y + 1))
            store(a, 16 * k + 8 * h, wx * along_x[h][a] + wy * along_y[h])


def sides_kernel(state_hbm, wx_hbm, wy_hbm, send_b_ref, send_a_ref, state, wx, wy, ends, sems):
    even = lax.axis_index("elem") % 2 == 0
    px = state_hbm.shape[0]
    copies = []
    for i, (element, x) in enumerate(((0, 0), (px - NP, px - 1))):
        copies.append(pltpu.make_async_copy(state_hbm.at[pl.ds(element, NP)], state.at[i], sems.at[i]))
        copies.append(pltpu.make_async_copy(wx_hbm.at[x], wx.at[i], sems.at[2 + i]))
        copies.append(pltpu.make_async_copy(wy_hbm.at[x], wy.at[i], sems.at[4 + i]))
    for copy in copies:
        copy.start()
    for copy in copies:
        copy.wait()
    for k in range(state.shape[2] // 16):
        for s, at in ((0, 0), (1, NP - 1)):
            def load(a, i):
                return state[s, a, i:i + 8, :]

            def store(a, i, value):
                ends[s, i:i + 8, :] = value

            tendency(k, (at,), load, lambda a, y: wx[s, y:y + 1, :], lambda a, y: wy[s, y:y + 1, :], store)
    send_a_ref[...] = jnp.where(even, ends[1], ends[0])
    send_b_ref[...] = jnp.where(even, ends[0], ends[1])


def smooth_rows(v, up, down):
    m0, n0 = half_coefs(0.5, 1.0), half_coefs(0.5, 0.0)
    m1, n1 = half_coefs(1.0, 0.5), half_coefs(0.0, 0.5)
    r = [pltpu.roll(piece, 4, axis=0) for piece in v]
    out = []
    for i in range(len(v)):
        if i % 2 == 0:
            other = r[i - 1] if i else up
            out.append(m0 * v[i] if other is None else m0 * v[i] + n0 * other)
        else:
            other = r[i + 1] if i < len(v) - 1 else down
            out.append(m1 * v[i] if other is None else m1 * v[i] + n1 * other)
    return out


def local_kernel(state, wx, wy, adv_hbm, tracer_ref, edge_ref, tend, adv, sems):
    elements = state.shape[0] // NP
    rows = state.shape[1]
    lower = iota((8, LEV), 0) < 4

    def out_copy(e):
        piece = pl.ds(e * NP, NP)
        return pltpu.make_async_copy(adv.at[piece], adv_hbm.at[piece], sems.at[e])

    def differentiate(e):
        def load(a, i):
            return state[e * NP + a, i:i + 8, :]

        def store(a, i, value):
            tend[e * NP + a, i:i + 8, :] = value

        for k in range(rows // 16):
            tendency(k, range(NP), load, lambda a, y: wx[e * NP + a, y:y + 1, :], lambda a, y: wy[e * NP + a, y:y + 1, :], store)

    def finish(e):
        for a in range(NP):
            x = e * NP + a
            v = [tend[x, 8 * i:8 * i + 8, :] for i in range(rows // 8)]
            if a == 0:
                left = jnp.maximum(x - 1, 0)
                share = jnp.where(e > 0, 0.5, 0.0).astype(F32)
                v = [0.5 * v[i] + share * tend[left, 8 * i:8 * i + 8, :] for i in range(rows // 8)]
            if a == NP - 1:
                right = jnp.minimum(x + 1, elements * NP - 1)
                share = jnp.where(e < elements - 1, 0.5, 0.0).astype(F32)
                v = [0.5 * v[i] + share * tend[right, 8 * i:8 * i + 8, :] for i in range(rows // 8)]
            edge_ref[x] = jnp.where(lower, v[0], v[-1])
            for i, value in enumerate(smooth_rows(v, None, None)):
                adv[x, 8 * i:8 * i + 8, :] = state[x, 8 * i:8 * i + 8, :] + value
            tracer_ref[x] = adv[x, pl.ds(1, rows // NT, stride=NT), :]
        out_copy(e).start()

    differentiate(0)

    def step(e, carry):
        differentiate(e)
        finish(e - 1)
        return carry

    lax.fori_loop(1, elements, step, 0)
    finish(elements - 1)
    for e in range(elements):
        out_copy(e).wait()


def edge_kernel(edge_ref, got_b_ref, got_a_ref, send_d_ref, send_c_ref, both):
    even = lax.axis_index("elem") % 2 == 0
    even_y = lax.axis_index("blk") % 2 == 0
    px = edge_ref.shape[0]
    rows = got_a_ref.shape[0]
    lower = iota((8, LEV), 0) < 4
    before = jnp.where(even, got_b_ref[...], got_a_ref[...])
    after = jnp.where(even, got_a_ref[...], got_b_ref[...])
    for x in range(px):
        both[8 * x:8 * x + 8, :] = edge_ref[x]
    for x, side in ((0, before), (px - 1, after)):
        both[8 * x:8 * x + 8, :] = edge_ref[x] + 0.5 * jnp.where(lower, side[0:8], side[rows - 8:rows])
    for t in range(NT):
        first = both[pl.ds(t, px, stride=8), :]
        final = both[pl.ds(NT + t, px, stride=8), :]
        send_c_ref[t * px:t * px + px, :] = jnp.where(even_y, final, first)
        send_d_ref[t * px:t * px + px, :] = jnp.where(even_y, first, final)


def side_shares(even, got_a_ref, got_b_ref, rows):
    before = [0.5 * jnp.where(even, got_b_ref[i:i + 8, :], got_a_ref[i:i + 8, :]) for i in range(0, rows, 8)]
    after = [0.5 * jnp.where(even, got_a_ref[i:i + 8, :], got_b_ref[i:i + 8, :]) for i in range(0, rows, 8)]
    return smooth_rows(before, None, None), smooth_rows(after, None, None)


def rain_place(half):
    lane = iota((half, LEV), 1)
    return (lane < 2 * half) & (lane % half == iota((half, LEV), 0))


def rain_row(part, place):
    sums = jnp.sum(part, axis=1, keepdims=True) * 0.125
    return jnp.sum(jnp.where(place, sums, 0.0), axis=0, keepdims=True)


def early_rain_kernel(tracer_ref, got_a_ref, got_b_ref, table_ref, rain_ref, side_ref):
    px, py, _ = tracer_ref.shape
    half = py // 2
    rows = py * NT
    for s, side in enumerate(side_shares(lax.axis_index("elem") % 2 == 0, got_a_ref, got_b_ref, rows)):
        for i, value in enumerate(side):
            side_ref[s, 8 * i:8 * i + 8, :] = value
    place = rain_place(half)

    def one(x, extra):
        for h in range(2):
            part = tracer_ref[x, half * h:half * h + half, :]
            if extra is not None:
                part = part + extra[half * h:half * h + half]
            at = pl.ds(h * px + x, 1)
            rain_ref[at, :] = rain_row(part * table_ref[at, :], place)

    for x in range(px):
        side = {0: 0, px - 1: 1}.get(x)
        one(x, None if side is None else side_ref[side, pl.ds(1, py, stride=NT), :])


def rain_kernel(costs_ref, bad_ref, tracer_ref, got_a_ref, got_b_ref, got_c_ref, got_d_ref, early_ref, table_ref, lanes_ref, onehot_ref, first_ref, second_ref, out_ref, rain_ref, side_ref):
    px, py, _ = tracer_ref.shape
    half = py // 2
    rows = py * NT
    groups = 2 * px
    even_y = lax.axis_index("blk") % 2 == 0
    up = 0.5 * jnp.where(even_y, got_d_ref[px:2 * px, :], got_c_ref[px:2 * px, :])
    down = 0.5 * jnp.where(even_y, got_c_ref[px:2 * px, :], got_d_ref[px:2 * px, :])

    lane = iota((groups, LEV), 1)

    def send(rain):
        values = jnp.where(lane == 2 * half, 1.0, jnp.where(lanes_ref[...] > 0.5, rain, 0.0))
        picked = exact_pick(onehot_ref[...], values)
        first, second = picked[:groups], picked[groups:]
        out_ref[...] = jnp.where(lane < half, first, jnp.where(lane < 2 * half, second, first + second))

    sums = jnp.sum(jnp.concatenate([up, down], axis=0) * table_ref[...], axis=1, keepdims=True) * 0.125
    column = jnp.where(iota((groups, LEV), 0) < px, 0, half - 1)
    send(early_ref[...] + jnp.where((lane == column) | (lane == column + half), sums, 0.0))
    bad = jnp.max(bad_ref[...]) > 0.5

    @pl.when(bad)
    def _():
        for s, side in enumerate(side_shares(lax.axis_index("elem") % 2 == 0, got_a_ref, got_b_ref, rows)):
            for i, value in enumerate(side):
                side_ref[s, 8 * i:8 * i + 8, :] = value
        rain_ref[0:px, :] = up
        rain_ref[px:2 * px, :] = down
        place = rain_place(half)
        row = iota((half, LEV), 0)

        def one(x, carry):
            near = jnp.where(x == 0, 1.0, 0.0).astype(F32)
            far = jnp.where(x == px - 1, 1.0, 0.0).astype(F32)
            for h, at in ((0, 0), (1, half - 1)):
                def side(s):
                    return side_ref[s, pl.ds(1 + half * NT * h, half, stride=NT), :]

                here = pl.ds(h * px + x, 1)
                part = tracer_ref[x, half * h:half * h + half, :] + (near * side(0) + far * side(1))
                part = part + jnp.where(row == at, rain_ref[here, :], 0.0)
                done = repeated(part, jnp.max(costs_ref[here, :]).astype(jnp.int32), first_ref, second_ref)
                rain_ref[here, :] = rain_row(part - done, place)
            return carry

        lax.fori_loop(0, px, one, 0)
        send(rain_ref[...])


def mix_kernel(cost_hbm, bad_hbm, mixing_hbm, trig_hbm, got_a_hbm, got_b_hbm, got_c_hbm, got_d_hbm, first_hbm, second_hbm, adv_hbm, new_hbm, adv, new, powers, cost_ref, bad_ref, mixing_ref, trig_ref, got_a_ref, got_b_ref, got_c_ref, got_d_ref, first_ref, second_ref, mask_ref, sems, out_sems, small_sems):
    px, rows, _ = adv.shape
    py = rows // NT
    half = rows // 2
    chunks = sems.shape[0]
    size = px // chunks
    out = px // out_sems.shape[0]
    even_y = lax.axis_index("blk") % 2 == 0
    lower = iota((8, LEV), 0) < 4

    def in_copy(i):
        return pltpu.make_async_copy(adv_hbm.at[pl.ds(i * size, size)], adv.at[pl.ds(i * size, size)], sems.at[i])

    def out_copy(i):
        return pltpu.make_async_copy(new.at[pl.ds(i * out, out)], new_hbm.at[pl.ds(i * out, out)], out_sems.at[i])

    small = [
        pltpu.make_async_copy(src, dst, small_sems.at[i])
        for i, (src, dst) in enumerate(
            (
                (mixing_hbm, mixing_ref),
                (bad_hbm, bad_ref),
                (cost_hbm, cost_ref),
                (trig_hbm, trig_ref),
                (got_a_hbm, got_a_ref),
                (got_b_hbm, got_b_ref),
                (got_c_hbm, got_c_ref),
                (got_d_hbm, got_d_ref),
                (first_hbm, first_ref),
                (second_hbm, second_ref),
            )
        )
    ]
    for copy in small:
        copy.start()
    for i in range(chunks):
        in_copy(i).start()
    small[0].wait()
    small[1].wait()
    bad = jnp.max(bad_ref[...]) > 0.5
    good = jnp.logical_not(bad)

    @pl.when(good)
    def _():
        powers[0] = jnp.concatenate(split3(mixing_ref[...].T), axis=1)

        def part(j):
            return powers[j, :, 0:LEV], powers[j, :, LEV:2 * LEV], powers[j, :, 2 * LEV:3 * LEV]

        for k in (1, 2, 4, 8):
            first, second = weights(*part(k - 1))

            def step(j, carry):
                powers[j + k] = jnp.concatenate(split3(precise(*part(j), first, second)), axis=1)
                return carry

            lax.fori_loop(0, k, step, 0, unroll=True)

        for k in (16, 32):
            pair = powers[k - 1, :, 0:2 * LEV]
            both = jnp.concatenate([pair, pair], axis=0)

            def later(j, carry):
                value = mm(powers[j, :, 0:2 * LEV], both)
                powers[j + k, :, 0:2 * LEV] = jnp.concatenate(split2(value[:, :LEV] + value[:, LEV:]), axis=1)
                return carry

            lax.fori_loop(0, k, later, 0, unroll=8)

    for copy in small[2:]:
        copy.wait()
    trig = jnp.concatenate([trig_ref[...].astype(F32), jnp.zeros((LEV - px, py), F32)], axis=0).T
    spread = jnp.where(iota((rows, py), 0) // NT == iota((rows, py), 1), 1.0, 0.0).astype(BF16)
    mask_ref[...] = mm(spread, trig.astype(BF16))
    shares = side_shares(lax.axis_index("elem") % 2 == 0, got_a_ref, got_b_ref, rows)
    in_copy(0).wait()
    in_copy(chunks - 1).wait()
    for x, share in ((0, shares[0]), (px - 1, shares[1])):
        for i in range(rows // 8):
            adv[x, 8 * i:8 * i + 8, :] = adv[x, 8 * i:8 * i + 8, :] + share[i]

    def edged(x, h):
        start = adv[x, half * h:half * h + half, :]
        at = pl.ds(x, NT, stride=px)
        if h == 0:
            add = 0.5 * jnp.where(even_y, got_d_ref[at, :], got_c_ref[at, :])
            return jnp.concatenate([start[0:8] + jnp.where(lower, jnp.concatenate([add, add], axis=0), 0.0), start[8:]], axis=0)
        add = 0.5 * jnp.where(even_y, got_c_ref[at, :], got_d_ref[at, :])
        return jnp.concatenate([start[:half - 8], start[half - 8:] + jnp.where(lower, 0.0, jnp.concatenate([add, add], axis=0))], axis=0)

    def powered(x, h, start):
        high, low = split2(start)
        both = mm(jnp.concatenate([high, low], axis=0), powers[cost_ref[2 * x + h] - 1, :, 0:2 * LEV])
        return (both[:half, :LEV] + both[half:, :LEV]) + (both[:half, LEV:] + both[half:, LEV:])

    def step_by_step(x, h, start):
        return repeated(start, cost_ref[2 * x + h], first_ref, second_ref)

    def one(rule, x, mask):
        for h in range(2):
            start = edged(x, h)
            done = rule(x, h, start)
            new[x, half * h:half * h + half, :] = jnp.where(mask[half * h:half * h + half] > 0.5, done, start)

    def arrive(i):
        @pl.when((i > 0) & (i < chunks - 1))
        def _():
            in_copy(i).wait()

    @pl.when(good)
    def _():
        def chunk(i, carry):
            arrive(i)
            rolled = pltpu.roll(mask_ref[...], lax.rem(LEV - i * size, LEV), axis=1)
            for a in range(size):
                one(powered, i * size + a, jnp.broadcast_to(rolled[:, a:a + 1], (rows, LEV)))
                if a % out == out - 1:
                    out_copy(i * (size // out) + a // out).start()
            return carry

        lax.fori_loop(0, chunks, chunk, 0)

    @pl.when(bad)
    def _():
        def chunk(i, carry):
            arrive(i)

            def column(a, carry):
                x = i * size + a
                rolled = pltpu.roll(mask_ref[...], lax.rem(LEV - x, LEV), axis=1)
                one(step_by_step, x, jnp.broadcast_to(rolled[:, 0:1], (rows, LEV)))
                return carry

            lax.fori_loop(0, size, column, 0)
            for j in range(size // out):
                out_copy(i * (size // out) + j).start()
            return carry

        lax.fori_loop(0, chunks, chunk, 0)

    for i in range(px // out):
        out_copy(i).wait()


def gather_kernel(got_ref, rain_ref):
    got = got_ref[...]
    size = got.shape
    half = GROUP_COLS
    count_col = jnp.sum(jnp.where(iota(size, 1) == 2 * half, got, 0.0), axis=1, keepdims=True)
    earlier = jnp.where(iota(size, 0) < iota(size, 1), count_col, 0.0)
    start = jnp.sum(earlier, axis=0, keepdims=True).astype(jnp.int32)
    count = jnp.sum(jnp.where(iota(size, 0) == iota(size, 1), count_col, 0.0), axis=0, keepdims=True).astype(jnp.int32)
    per = LEV // half
    rows = size[0] // per
    slot = (iota(size, 0) % rows) * per + iota(size, 0) // rows
    pick0 = jnp.where((slot == start) & (count > 0), 1.0, 0.0)
    pick1 = jnp.where((slot == start + 1) & (count > 1), 1.0, 0.0)
    picked = exact_pick(jnp.concatenate([pick0, pick1], axis=0).astype(BF16), got)
    lane = iota((rows, LEV), 1)
    first, second = picked[:size[0]], pltpu.roll(picked[size[0]:], LEV - half, axis=1)
    total = jnp.where(iota(size, 1) < half, first + second, 0.0)
    out = total[0:rows]
    for q in range(1, per):
        out = jnp.where(lane // half == q, pltpu.roll(total[q * rows:(q + 1) * rows], half * q, axis=1), out)
    rain_ref[...] = out


VMEM = pl.BlockSpec(memory_space=pltpu.VMEM)
HBM = pl.BlockSpec(memory_space=pltpu.HBM)


def params(mib):
    return pltpu.CompilerParams(vmem_limit_bytes=mib * MIB)


def cost(flops, moved):
    return pl.CostEstimate(flops=flops, bytes_accessed=moved, transcendentals=0)


def body(state, wind_x, wind_y, mixing, triggers, group_costs, destinations):
    px, py, nt, lev = state.shape
    rows = py * nt
    groups = group_costs.shape[0]
    elements = px // NP
    n_elem, n_blk = lax.axis_size("elem"), lax.axis_size("blk")
    slabs = state.reshape(px, rows, lev)
    def struct(*shape, dtype=F32):
        return jax.ShapeDtypeStruct(shape, dtype)

    def block(shape, *at):
        return pl.BlockSpec(shape, lambda i: at)

    def kept(x):
        return pltpu.with_memory_space_constraint(x, pltpu.HBM)

    send_b, send_a = pl.pallas_call(
        sides_kernel,
        out_shape=(struct(rows, lev),) * 2,
        in_specs=[HBM] * 3,
        out_specs=(VMEM, VMEM),
        scratch_shapes=[
            pltpu.VMEM((2, NP, rows, lev), F32),
            pltpu.VMEM((2, py, lev), F32),
            pltpu.VMEM((2, py, lev), F32),
            pltpu.VMEM((2, rows, lev), F32),
            pltpu.SemaphoreType.DMA((6,)),
        ],
        compiler_params=params(4),
        cost_estimate=cost(2 * MIB, MIB),
        name="sides",
    )(kept(slabs), kept(wind_x), kept(wind_y))

    pair_a = [(i, i ^ 1) for i in range(n_elem)]
    pair_b = [(i, (i - 1 if i % 2 == 0 else i + 1) % n_elem) for i in range(n_elem)]
    pair_c = [(j, j ^ 1) for j in range(n_blk)]
    pair_d = [(j, (j - 1 if j % 2 == 0 else j + 1) % n_blk) for j in range(n_blk)]
    got_b = lax.ppermute(send_b, "elem", pair_b)
    got_a = lax.ppermute(send_a, "elem", pair_a)

    local, tracer, edges = pl.pallas_call(
        local_kernel,
        out_shape=(pltpu.HBM((px, rows, lev), F32), struct(px, py, lev), struct(px, 8, lev)),
        in_specs=[VMEM, VMEM, VMEM],
        out_specs=(HBM, VMEM, VMEM),
        scratch_shapes=[
            pltpu.VMEM((px, rows, lev), F32),
            pltpu.VMEM((px, rows, lev), F32),
            pltpu.SemaphoreType.DMA((elements,)),
        ],
        compiler_params=params(14),
        cost_estimate=cost(64 * MIB, 12 * MIB),
        name="local",
    )(slabs, wind_x, wind_y)

    send_d, send_c = pl.pallas_call(
        edge_kernel,
        out_shape=(struct(nt * px, lev),) * 2,
        in_specs=[VMEM, VMEM, VMEM],
        out_specs=(VMEM, VMEM),
        scratch_shapes=[pltpu.VMEM((8 * px, lev), F32)],
        compiler_params=params(8),
        cost_estimate=cost(MIB, MIB),
        name="edges",
    )(edges, got_b, got_a)
    got_d = lax.ppermute(send_d, "blk", pair_d)
    got_c = lax.ppermute(send_c, "blk", pair_c)

    table, onehots, lanes, costs, first, second, bad = pl.pallas_call(
        gains_kernel,
        out_shape=(
            struct(groups, lev),
            struct(2 * groups, groups, dtype=BF16),
            struct(groups, lev),
            struct(groups, lev),
            struct(2 * lev, 2 * lev, dtype=BF16),
            struct(2 * lev, lev, dtype=BF16),
            struct(8, lev),
        ),
        in_specs=[VMEM] * 4,
        out_specs=(VMEM,) * 7,
        scratch_shapes=[pltpu.VMEM((MAXC, lev), F32)],
        compiler_params=params(8),
        cost_estimate=cost(512 * MIB, MIB),
        name="gains",
    )(mixing, destinations.reshape(1, groups), group_costs.reshape(1, groups), triggers)

    early = pl.pallas_call(
        early_rain_kernel,
        out_shape=struct(groups, lev),
        in_specs=[VMEM] * 4,
        out_specs=VMEM,
        scratch_shapes=[pltpu.VMEM((2, rows, lev), F32)],
        compiler_params=params(8),
        cost_estimate=cost(512 * MIB, MIB),
        name="early_rain",
    )(tracer, got_a, got_b, table)

    outgoing = pl.pallas_call(
        rain_kernel,
        out_shape=struct(groups, lev),
        in_specs=[VMEM] * 13,
        out_specs=VMEM,
        scratch_shapes=[pltpu.VMEM((groups, lev), F32), pltpu.VMEM((2, rows, lev), F32)],
        compiler_params=params(12),
        cost_estimate=cost(64 * MIB, 2 * MIB),
        name="rain",
    )(costs, bad, tracer, got_a, got_b, got_c, got_d, early, table, lanes, onehots, first, second)

    incoming = lax.all_to_all(outgoing, ("elem", "blk"), split_axis=0, concat_axis=0, tiled=True)

    chunks = 4
    new = pl.pallas_call(
        mix_kernel,
        out_shape=struct(px, rows, lev),
        in_specs=[HBM] * 11,
        out_specs=HBM,
        scratch_shapes=[
            pltpu.VMEM((px, rows, lev), F32),
            pltpu.VMEM((px, rows, lev), F32),
            pltpu.VMEM((MAXC, lev, 3 * lev), BF16),
            pltpu.SMEM((groups,), jnp.int32),
            pltpu.VMEM((8, lev), F32),
            pltpu.VMEM((lev, lev), F32),
            pltpu.VMEM((px, py), jnp.int32),
            pltpu.VMEM((rows, lev), F32),
            pltpu.VMEM((rows, lev), F32),
            pltpu.VMEM((nt * px, lev), F32),
            pltpu.VMEM((nt * px, lev), F32),
            pltpu.VMEM((2 * lev, 2 * lev), BF16),
            pltpu.VMEM((2 * lev, lev), BF16),
            pltpu.VMEM((rows, lev), F32),
            pltpu.SemaphoreType.DMA((chunks,)),
            pltpu.SemaphoreType.DMA((2 * chunks,)),
            pltpu.SemaphoreType.DMA((10,)),
        ],
        compiler_params=params(60),
        cost_estimate=cost(4096 * MIB, 10 * MIB),
        name="mix",
    )(group_costs, bad, mixing, triggers, got_a, got_b, got_c, got_d, first, second, kept(local))

    rain = pl.pallas_call(
        gather_kernel,
        out_shape=struct(groups * GROUP_COLS // lev, lev),
        in_specs=[VMEM],
        out_specs=VMEM,
        compiler_params=params(8),
        cost_estimate=cost(MIB, MIB),
        name="gather",
    )(incoming)
    return new.reshape(state.shape), rain.reshape(-1)


def solution(mesh):
    return jax.shard_map(
        body,
        mesh=mesh,
        in_specs=(
            P("elem", "blk", None, None),
            P("elem", "blk", None),
            P("elem", "blk", None),
            P(),
            P("elem", "blk"),
            P(("elem", "blk")),
            P(("elem", "blk")),
        ),
        out_specs=(P("elem", "blk", None, None), P(("elem", "blk"))),
        check_vma=False,
    )
```

```python
import functools

import jax
import jax.numpy as jnp
import numpy as np
from jax import lax
from jax.experimental import pallas as pl
from jax.experimental.pallas import tpu as pltpu
from jax.sharding import PartitionSpec as P

NP = 4
NT = 4
LEV = 128
GROUP_COLS = 16
MAXC = 64
LIMIT = 1.0e3
F32 = jnp.float32
BF16 = jnp.bfloat16
MIB = 1024 * 1024


def gll_derivative():
    nodes = np.array([-1.0, -1.0 / np.sqrt(5.0), 1.0 / np.sqrt(5.0), 1.0])
    legendre = (5.0 * nodes * nodes * nodes - 3.0 * nodes) / 2.0
    derivative = np.zeros((4, 4))
    for a in range(4):
        for b in range(4):
            if a != b:
                derivative[a, b] = legendre[a] / (legendre[b] * (nodes[a] - nodes[b]))
    derivative[0, 0] = -3.0
    derivative[3, 3] = 3.0
    return derivative


def split2(x):
    high = x.astype(BF16)
    return high, (x - high.astype(F32)).astype(BF16)


def split3(x):
    high = x.astype(BF16)
    rest = x - high.astype(F32)
    mid = rest.astype(BF16)
    return high, mid, (rest - mid.astype(F32)).astype(BF16)


def mm(a, b):
    return jnp.dot(a, b, preferred_element_type=F32)


def exact_pick(onehot, values):
    return mm(jnp.concatenate([onehot] * 3, axis=1), jnp.concatenate(split3(values), axis=0))


def weights(high, mid, low):
    pair = jnp.concatenate([high, mid], axis=1)
    return jnp.concatenate([pair, pair], axis=0), jnp.concatenate([low, high], axis=0)


def precise(high, mid, low, first, second):
    one = mm(jnp.concatenate([high, mid], axis=1), first)
    two = mm(jnp.concatenate([high, low], axis=1), second)
    return one[:, :LEV] + (one[:, LEV:] + two)


def repeated(start, cost, first_ref, second_ref):
    return lax.fori_loop(0, cost, lambda i, c: precise(*split3(c), first_ref[...], second_ref[...]), start)


def iota(shape, dim):
    return lax.broadcasted_iota(jnp.int32, shape, dim)


def gains_kernel(mixing_ref, dest_ref, cost_ref, trig_ref, table_ref, onehot_ref, lanes_ref, costs_ref, first_ref, second_ref, bad_ref, sums):
    square = mixing_ref[...]
    worst = jnp.max(jnp.abs(square))
    first_ref[...], second_ref[...] = weights(*split3(square.T))
    sums[0:8] = jnp.broadcast_to(jnp.sum(square, axis=0, keepdims=True), (8, LEV))
    for k in (1, 2, 4, 8, 16, 32):
        parts = split3(square)
        pair = weights(*parts)
        rows = max(k, 8)
        grown = precise(*split3(sums[0:rows]), *pair)
        if k < 8:
            pick = iota((8, LEV), 0)
            merged = sums[0:8]
            for j in range(k):
                merged = jnp.where(pick == j + k, grown[j:j + 1], merged)
            sums[0:8] = merged
        else:
            sums[k:2 * k] = grown
        if k < 32:
            square = precise(*parts, *pair)
            worst = jnp.maximum(worst, jnp.max(jnp.abs(square)))
    bad_ref[...] = jnp.full(bad_ref.shape, jnp.where(worst <= LIMIT, 0.0, 1.0), F32)

    px, py = trig_ref.shape
    half = py // 2
    groups = 2 * px
    shape = (groups, groups)
    first_at, second_at = iota(shape, 0), iota(shape, 1)
    number0 = 2 * (first_at % px) + first_at // px
    number1 = 2 * (second_at % px) + second_at // px
    diagonal = first_at == number1

    def across(row):
        return jnp.sum(jnp.where(first_at == second_at, row, 0), axis=1, keepdims=True)

    def ordered(row_ref):
        col = across(jnp.broadcast_to(row_ref[...], shape))
        return jnp.sum(jnp.where(diagonal, col, 0), axis=0, keepdims=True)

    dest_row = jnp.broadcast_to(ordered(dest_ref), shape)
    dest_col = across(dest_row)
    earlier = (dest_col == dest_row) & (number0 < number1)
    within = jnp.sum(jnp.where(earlier, 1, 0), axis=0, keepdims=True)
    at = dest_row == first_at
    onehot_ref[0:groups] = jnp.where(at & (within == 0), 1.0, 0.0).astype(BF16)
    onehot_ref[groups:2 * groups] = jnp.where(at & (within == 1), 1.0, 0.0).astype(BF16)

    cost_col = across(jnp.broadcast_to(ordered(cost_ref), shape))
    chosen = jnp.where(cost_col == iota((groups, MAXC), 1) + 1, 1.0, 0.0).astype(BF16)
    table_ref[...] = exact_pick(chosen, 1.0 - sums[...])
    costs_ref[...] = jnp.broadcast_to(cost_col, (groups, LEV)).astype(F32)

    wide = trig_ref[...].astype(F32).astype(BF16)
    lane = iota((py, LEV), 1)
    for h in range(2):
        placed = jnp.where((lane < 2 * half) & (lane % half + half * h == iota((py, LEV), 0)), 1.0, 0.0).astype(BF16)
        lanes_ref[h * px:h * px + px] = mm(wide, placed)


def half_coefs(first, second):
    return jnp.where(iota((8, LEV), 0) < 4, F32(first), F32(second))


def derivative_tables():
    deriv = -0.05 * gll_derivative()
    even = [float(np.float32(0.5 * (deriv[a, 0] + deriv[a, 3]))) for a in range(2)]
    odd = [[float(np.float32(0.5 * (deriv[a, b] - deriv[a, 3 - b]))) for b in range(2)] for a in range(2)]
    return even, odd


def tendency(k, points, load, load_x, load_y, store):
    even, odd = derivative_tables()
    c_even = half_coefs(even[0], -even[1])
    c_odd, c_cross = half_coefs(odd[0][0], odd[1][1]), half_coefs(odd[0][1], odd[1][0])
    lower = iota((8, LEV), 0) < 4
    v = [[load(a, 16 * k + 8 * h) for h in range(2)] for a in range(NP)]
    along_x = []
    for h in range(2):
        d0, d1 = v[0][h] - v[3][h], v[1][h] - v[2][h]
        mean = (v[0][h] + v[3][h]) - (v[1][h] + v[2][h])
        p0, p1 = even[0] * mean, even[1] * mean
        q0, q1 = odd[0][0] * d0 + odd[0][1] * d1, odd[1][0] * d0 + odd[1][1] * d1
        along_x.append((q0 + p0, q1 + p1, q1 - p1, q0 - p0))
    for a in points:
        r1 = pltpu.roll(v[a][1], 4, axis=0)
        add, sub = v[a][0] + r1, v[a][0] - r1
        odds = c_odd * sub + c_cross * pltpu.roll(sub, 4, axis=0)
        evens = c_even * (add - pltpu.roll(add, 4, axis=0))
        along_y = (odds + evens, pltpu.roll(odds - evens, 4, axis=0))
        for h in range(2):
            y = 4 * k + 2 * h
            wx = jnp.where(lower, load_x(a, y), load_x(a, y + 1))
            wy = jnp.where(lower, load_y(a, y), load_y(a, y + 1))
            store(a, 16 * k + 8 * h, wx * along_x[h][a] + wy * along_y[h])


def sides_kernel(state_hbm, wx_hbm, wy_hbm, send_b_ref, send_a_ref, state, wx, wy, ends, sems):
    even = lax.axis_index("elem") % 2 == 0
    px = state_hbm.shape[0]
    copies = []
    for i, (element, x) in enumerate(((0, 0), (px - NP, px - 1))):
        copies.append(pltpu.make_async_copy(state_hbm.at[pl.ds(element, NP)], state.at[i], sems.at[i]))
        copies.append(pltpu.make_async_copy(wx_hbm.at[x], wx.at[i], sems.at[2 + i]))
        copies.append(pltpu.make_async_copy(wy_hbm.at[x], wy.at[i], sems.at[4 + i]))
    for copy in copies:
        copy.start()
    for copy in copies:
        copy.wait()
    for k in range(state.shape[2] // 16):
        for s, at in ((0, 0), (1, NP - 1)):
            def load(a, i):
                return state[s, a, i:i + 8, :]

            def store(a, i, value):
                ends[s, i:i + 8, :] = value

            tendency(k, (at,), load, lambda a, y: wx[s, y:y + 1, :], lambda a, y: wy[s, y:y + 1, :], store)
    send_a_ref[...] = jnp.where(even, ends[1], ends[0])
    send_b_ref[...] = jnp.where(even, ends[0], ends[1])


def smooth_rows(v, up, down):
    m0, n0 = half_coefs(0.5, 1.0), half_coefs(0.5, 0.0)
    m1, n1 = half_coefs(1.0, 0.5), half_coefs(0.0, 0.5)
    r = [pltpu.roll(piece, 4, axis=0) for piece in v]
    out = []
    for i in range(len(v)):
        if i % 2 == 0:
            other = r[i - 1] if i else up
            out.append(m0 * v[i] if other is None else m0 * v[i] + n0 * other)
        else:
            other = r[i + 1] if i < len(v) - 1 else down
            out.append(m1 * v[i] if other is None else m1 * v[i] + n1 * other)
    return out


def local_kernel(state, wx, wy, adv_hbm, tracer_ref, edge_ref, tend, adv, sems):
    elements = state.shape[0] // NP
    rows = state.shape[1]
    lower = iota((8, LEV), 0) < 4

    def out_copy(e):
        piece = pl.ds(e * NP, NP)
        return pltpu.make_async_copy(adv.at[piece], adv_hbm.at[piece], sems.at[e])

    def differentiate(e):
        def load(a, i):
            return state[e * NP + a, i:i + 8, :]

        def store(a, i, value):
            tend[e * NP + a, i:i + 8, :] = value

        for k in range(rows // 16):
            tendency(k, range(NP), load, lambda a, y: wx[e * NP + a, y:y + 1, :], lambda a, y: wy[e * NP + a, y:y + 1, :], store)

    def finish(e):
        for a in range(NP):
            x = e * NP + a
            v = [tend[x, 8 * i:8 * i + 8, :] for i in range(rows // 8)]
            if a == 0:
                left = jnp.maximum(x - 1, 0)
                share = jnp.where(e > 0, 0.5, 0.0).astype(F32)
                v = [0.5 * v[i] + share * tend[left, 8 * i:8 * i + 8, :] for i in range(rows // 8)]
            if a == NP - 1:
                right = jnp.minimum(x + 1, elements * NP - 1)
                share = jnp.where(e < elements - 1, 0.5, 0.0).astype(F32)
                v = [0.5 * v[i] + share * tend[right, 8 * i:8 * i + 8, :] for i in range(rows // 8)]
            edge_ref[x] = jnp.where(lower, v[0], v[-1])
            for i, value in enumerate(smooth_rows(v, None, None)):
                adv[x, 8 * i:8 * i + 8, :] = state[x, 8 * i:8 * i + 8, :] + value
        out_copy(e).start()

    differentiate(0)

    def step(e, carry):
        differentiate(e)
        finish(e - 1)
        return carry

    lax.fori_loop(1, elements, step, 0)
    finish(elements - 1)
    for x in range(elements * NP):
        tracer_ref[x] = adv[x, pl.ds(1, rows // NT, stride=NT), :]
    for e in range(elements):
        out_copy(e).wait()


def edge_kernel(edge_ref, got_b_ref, got_a_ref, send_d_ref, send_c_ref, both):
    even = lax.axis_index("elem") % 2 == 0
    even_y = lax.axis_index("blk") % 2 == 0
    px = edge_ref.shape[0]
    rows = got_a_ref.shape[0]
    lower = iota((8, LEV), 0) < 4
    before = jnp.where(even, got_b_ref[...], got_a_ref[...])
    after = jnp.where(even, got_a_ref[...], got_b_ref[...])
    for x in range(px):
        both[8 * x:8 * x + 8, :] = edge_ref[x]
    for x, side in ((0, before), (px - 1, after)):
        both[8 * x:8 * x + 8, :] = edge_ref[x] + 0.5 * jnp.where(lower, side[0:8], side[rows - 8:rows])
    for t in range(NT):
        first = both[pl.ds(t, px, stride=8), :]
        final = both[pl.ds(NT + t, px, stride=8), :]
        send_c_ref[t * px:t * px + px, :] = jnp.where(even_y, final, first)
        send_d_ref[t * px:t * px + px, :] = jnp.where(even_y, first, final)


def side_shares(even, got_a_ref, got_b_ref, rows):
    before = [0.5 * jnp.where(even, got_b_ref[i:i + 8, :], got_a_ref[i:i + 8, :]) for i in range(0, rows, 8)]
    after = [0.5 * jnp.where(even, got_a_ref[i:i + 8, :], got_b_ref[i:i + 8, :]) for i in range(0, rows, 8)]
    return smooth_rows(before, None, None), smooth_rows(after, None, None)


def rain_place(half):
    lane = iota((half, LEV), 1)
    return (lane < 2 * half) & (lane % half == iota((half, LEV), 0))


def rain_row(part, place):
    sums = jnp.sum(part, axis=1, keepdims=True) * 0.125
    return jnp.sum(jnp.where(place, sums, 0.0), axis=0, keepdims=True)


def early_rain_kernel(tracer_ref, got_a_ref, got_b_ref, table_ref, rain_ref, side_ref):
    px, py, _ = tracer_ref.shape
    half = py // 2
    rows = py * NT
    for s, side in enumerate(side_shares(lax.axis_index("elem") % 2 == 0, got_a_ref, got_b_ref, rows)):
        for i, value in enumerate(side):
            side_ref[s, 8 * i:8 * i + 8, :] = value
    place = rain_place(half)

    def one(x, extra):
        for h in range(2):
            part = tracer_ref[x, half * h:half * h + half, :]
            if extra is not None:
                part = part + extra[half * h:half * h + half]
            at = pl.ds(h * px + x, 1)
            rain_ref[at, :] = rain_row(part * table_ref[at, :], place)

    for x in range(px):
        side = {0: 0, px - 1: 1}.get(x)
        one(x, None if side is None else side_ref[side, pl.ds(1, py, stride=NT), :])


def rain_kernel(costs_ref, bad_ref, tracer_ref, got_a_ref, got_b_ref, got_c_ref, got_d_ref, early_ref, table_ref, lanes_ref, onehot_ref, first_ref, second_ref, out_ref, rain_ref, side_ref):
    px, py, _ = tracer_ref.shape
    half = py // 2
    rows = py * NT
    groups = 2 * px
    even_y = lax.axis_index("blk") % 2 == 0
    up = 0.5 * jnp.where(even_y, got_d_ref[px:2 * px, :], got_c_ref[px:2 * px, :])
    down = 0.5 * jnp.where(even_y, got_c_ref[px:2 * px, :], got_d_ref[px:2 * px, :])

    lane = iota((groups, LEV), 1)

    def send(rain):
        values = jnp.where(lane == 2 * half, 1.0, jnp.where(lanes_ref[...] > 0.5, rain, 0.0))
        picked = exact_pick(onehot_ref[...], values)
        first, second = picked[:groups], picked[groups:]
        out_ref[...] = jnp.where(lane < half, first, jnp.where(lane < 2 * half, second, first + second))

    sums = jnp.sum(jnp.concatenate([up, down], axis=0) * table_ref[...], axis=1, keepdims=True) * 0.125
    column = jnp.where(iota((groups, LEV), 0) < px, 0, half - 1)
    send(early_ref[...] + jnp.where((lane == column) | (lane == column + half), sums, 0.0))
    bad = jnp.max(bad_ref[...]) > 0.5

    @pl.when(bad)
    def _():
        for s, side in enumerate(side_shares(lax.axis_index("elem") % 2 == 0, got_a_ref, got_b_ref, rows)):
            for i, value in enumerate(side):
                side_ref[s, 8 * i:8 * i + 8, :] = value
        rain_ref[0:px, :] = up
        rain_ref[px:2 * px, :] = down
        place = rain_place(half)
        row = iota((half, LEV), 0)

        def one(x, carry):
            near = jnp.where(x == 0, 1.0, 0.0).astype(F32)
            far = jnp.where(x == px - 1, 1.0, 0.0).astype(F32)
            for h, at in ((0, 0), (1, half - 1)):
                def side(s):
                    return side_ref[s, pl.ds(1 + half * NT * h, half, stride=NT), :]

                here = pl.ds(h * px + x, 1)
                part = tracer_ref[x, half * h:half * h + half, :] + (near * side(0) + far * side(1))
                part = part + jnp.where(row == at, rain_ref[here, :], 0.0)
                done = repeated(part, jnp.max(costs_ref[here, :]).astype(jnp.int32), first_ref, second_ref)
                rain_ref[here, :] = rain_row(part - done, place)
            return carry

        lax.fori_loop(0, px, one, 0)
        send(rain_ref[...])


def mix_kernel(cost_hbm, bad_hbm, mixing_hbm, trig_hbm, got_a_hbm, got_b_hbm, got_c_hbm, got_d_hbm, first_hbm, second_hbm, adv_hbm, new_hbm, adv, new, powers, cost_ref, bad_ref, mixing_ref, trig_ref, got_a_ref, got_b_ref, got_c_ref, got_d_ref, first_ref, second_ref, mask_ref, sems, out_sems, small_sems):
    px, rows, _ = adv.shape
    py = rows // NT
    half = rows // 2
    chunks = sems.shape[0]
    size = px // chunks
    out = px // out_sems.shape[0]
    even_y = lax.axis_index("blk") % 2 == 0
    lower = iota((8, LEV), 0) < 4

    def in_copy(i):
        return pltpu.make_async_copy(adv_hbm.at[pl.ds(i * size, size)], adv.at[pl.ds(i * size, size)], sems.at[i])

    def out_copy(i):
        return pltpu.make_async_copy(new.at[pl.ds(i * out, out)], new_hbm.at[pl.ds(i * out, out)], out_sems.at[i])

    small = [
        pltpu.make_async_copy(src, dst, small_sems.at[i])
        for i, (src, dst) in enumerate(
            (
                (mixing_hbm, mixing_ref),
                (bad_hbm, bad_ref),
                (cost_hbm, cost_ref),
                (trig_hbm, trig_ref),
                (got_a_hbm, got_a_ref),
                (got_b_hbm, got_b_ref),
                (got_c_hbm, got_c_ref),
                (got_d_hbm, got_d_ref),
                (first_hbm, first_ref),
                (second_hbm, second_ref),
            )
        )
    ]
    for copy in small:
        copy.start()
    for i in range(chunks):
        in_copy(i).start()
    small[0].wait()
    small[1].wait()
    bad = jnp.max(bad_ref[...]) > 0.5
    good = jnp.logical_not(bad)

    @pl.when(good)
    def _():
        powers[0] = jnp.concatenate(split3(mixing_ref[...].T), axis=1)

        def part(j):
            return powers[j, :, 0:LEV], powers[j, :, LEV:2 * LEV], powers[j, :, 2 * LEV:3 * LEV]

        for k in (1, 2, 4, 8):
            first, second = weights(*part(k - 1))

            def step(j, carry):
                powers[j + k] = jnp.concatenate(split3(precise(*part(j), first, second)), axis=1)
                return carry

            lax.fori_loop(0, k, step, 0, unroll=True)

        for k in (16, 32):
            pair = powers[k - 1, :, 0:2 * LEV]
            both = jnp.concatenate([pair, pair], axis=0)

            def later(j, carry):
                value = mm(powers[j, :, 0:2 * LEV], both)
                powers[j + k, :, 0:2 * LEV] = jnp.concatenate(split2(value[:, :LEV] + value[:, LEV:]), axis=1)
                return carry

            lax.fori_loop(0, k, later, 0, unroll=8)

    for copy in small[2:]:
        copy.wait()
    trig = jnp.concatenate([trig_ref[...].astype(F32), jnp.zeros((LEV - px, py), F32)], axis=0).T
    spread = jnp.where(iota((rows, py), 0) // NT == iota((rows, py), 1), 1.0, 0.0).astype(BF16)
    mask_ref[...] = mm(spread, trig.astype(BF16))
    shares = side_shares(lax.axis_index("elem") % 2 == 0, got_a_ref, got_b_ref, rows)
    in_copy(0).wait()
    in_copy(chunks - 1).wait()
    for x, share in ((0, shares[0]), (px - 1, shares[1])):
        for i in range(rows // 8):
            adv[x, 8 * i:8 * i + 8, :] = adv[x, 8 * i:8 * i + 8, :] + share[i]

    def edged(x, h):
        start = adv[x, half * h:half * h + half, :]
        at = pl.ds(x, NT, stride=px)
        if h == 0:
            add = 0.5 * jnp.where(even_y, got_d_ref[at, :], got_c_ref[at, :])
            return jnp.concatenate([start[0:8] + jnp.where(lower, jnp.concatenate([add, add], axis=0), 0.0), start[8:]], axis=0)
        add = 0.5 * jnp.where(even_y, got_c_ref[at, :], got_d_ref[at, :])
        return jnp.concatenate([start[:half - 8], start[half - 8:] + jnp.where(lower, 0.0, jnp.concatenate([add, add], axis=0))], axis=0)

    def powered(x, h, start):
        high, low = split2(start)
        both = mm(jnp.concatenate([high, low], axis=0), powers[cost_ref[2 * x + h] - 1, :, 0:2 * LEV])
        return (both[:half, :LEV] + both[half:, :LEV]) + (both[:half, LEV:] + both[half:, LEV:])

    def step_by_step(x, h, start):
        return repeated(start, cost_ref[2 * x + h], first_ref, second_ref)

    def one(rule, x, mask):
        for h in range(2):
            start = edged(x, h)
            done = rule(x, h, start)
            new[x, half * h:half * h + half, :] = jnp.where(mask[half * h:half * h + half] > 0.5, done, start)

    def arrive(i):
        @pl.when((i > 0) & (i < chunks - 1))
        def _():
            in_copy(i).wait()

    @pl.when(good)
    def _():
        def chunk(i, carry):
            arrive(i)
            rolled = pltpu.roll(mask_ref[...], lax.rem(LEV - i * size, LEV), axis=1)
            for a in range(size):
                one(powered, i * size + a, jnp.broadcast_to(rolled[:, a:a + 1], (rows, LEV)))
                if a % out == out - 1:
                    out_copy(i * (size // out) + a // out).start()
            return carry

        lax.fori_loop(0, chunks, chunk, 0)

    @pl.when(bad)
    def _():
        def chunk(i, carry):
            arrive(i)

            def column(a, carry):
                x = i * size + a
                rolled = pltpu.roll(mask_ref[...], lax.rem(LEV - x, LEV), axis=1)
                one(step_by_step, x, jnp.broadcast_to(rolled[:, 0:1], (rows, LEV)))
                return carry

            lax.fori_loop(0, size, column, 0)
            for j in range(size // out):
                out_copy(i * (size // out) + j).start()
            return carry

        lax.fori_loop(0, chunks, chunk, 0)

    for i in range(px // out):
        out_copy(i).wait()


def gather_kernel(got_ref, rain_ref):
    got = got_ref[...]
    size = got.shape
    half = GROUP_COLS
    count_col = jnp.sum(jnp.where(iota(size, 1) == 2 * half, got, 0.0), axis=1, keepdims=True)
    earlier = jnp.where(iota(size, 0) < iota(size, 1), count_col, 0.0)
    start = jnp.sum(earlier, axis=0, keepdims=True).astype(jnp.int32)
    count = jnp.sum(jnp.where(iota(size, 0) == iota(size, 1), count_col, 0.0), axis=0, keepdims=True).astype(jnp.int32)
    per = LEV // half
    rows = size[0] // per
    slot = (iota(size, 0) % rows) * per + iota(size, 0) // rows
    pick0 = jnp.where((slot == start) & (count > 0), 1.0, 0.0)
    pick1 = jnp.where((slot == start + 1) & (count > 1), 1.0, 0.0)
    picked = exact_pick(jnp.concatenate([pick0, pick1], axis=0).astype(BF16), got)
    lane = iota((rows, LEV), 1)
    first, second = picked[:size[0]], pltpu.roll(picked[size[0]:], LEV - half, axis=1)
    total = jnp.where(iota(size, 1) < half, first + second, 0.0)
    out = total[0:rows]
    for q in range(1, per):
        out = jnp.where(lane // half == q, pltpu.roll(total[q * rows:(q + 1) * rows], half * q, axis=1), out)
    rain_ref[...] = out


VMEM = pl.BlockSpec(memory_space=pltpu.VMEM)
HBM = pl.BlockSpec(memory_space=pltpu.HBM)


def params(mib):
    return pltpu.CompilerParams(vmem_limit_bytes=mib * MIB)


def cost(flops, moved):
    return pl.CostEstimate(flops=flops, bytes_accessed=moved, transcendentals=0)


def body(state, wind_x, wind_y, mixing, triggers, group_costs, destinations):
    px, py, nt, lev = state.shape
    rows = py * nt
    groups = group_costs.shape[0]
    elements = px // NP
    n_elem, n_blk = lax.axis_size("elem"), lax.axis_size("blk")
    slabs = state.reshape(px, rows, lev)
    def struct(*shape, dtype=F32):
        return jax.ShapeDtypeStruct(shape, dtype)

    def block(shape, *at):
        return pl.BlockSpec(shape, lambda i: at)

    def kept(x):
        return pltpu.with_memory_space_constraint(x, pltpu.HBM)

    send_b, send_a = pl.pallas_call(
        sides_kernel,
        out_shape=(struct(rows, lev),) * 2,
        in_specs=[HBM] * 3,
        out_specs=(VMEM, VMEM),
        scratch_shapes=[
            pltpu.VMEM((2, NP, rows, lev), F32),
            pltpu.VMEM((2, py, lev), F32),
            pltpu.VMEM((2, py, lev), F32),
            pltpu.VMEM((2, rows, lev), F32),
            pltpu.SemaphoreType.DMA((6,)),
        ],
        compiler_params=params(4),
        cost_estimate=cost(2 * MIB, MIB),
        name="sides",
    )(kept(slabs), kept(wind_x), kept(wind_y))

    pair_a = [(i, i ^ 1) for i in range(n_elem)]
    pair_b = [(i, (i - 1 if i % 2 == 0 else i + 1) % n_elem) for i in range(n_elem)]
    pair_c = [(j, j ^ 1) for j in range(n_blk)]
    pair_d = [(j, (j - 1 if j % 2 == 0 else j + 1) % n_blk) for j in range(n_blk)]
    got_b = lax.ppermute(send_b, "elem", pair_b)
    got_a = lax.ppermute(send_a, "elem", pair_a)

    local, tracer, edges = pl.pallas_call(
        local_kernel,
        out_shape=(pltpu.HBM((px, rows, lev), F32), struct(px, py, lev), struct(px, 8, lev)),
        in_specs=[VMEM, VMEM, VMEM],
        out_specs=(HBM, VMEM, VMEM),
        scratch_shapes=[
            pltpu.VMEM((px, rows, lev), F32),
            pltpu.VMEM((px, rows, lev), F32),
            pltpu.SemaphoreType.DMA((elements,)),
        ],
        compiler_params=params(14),
        cost_estimate=cost(64 * MIB, 12 * MIB),
        name="local",
    )(slabs, wind_x, wind_y)

    send_d, send_c = pl.pallas_call(
        edge_kernel,
        out_shape=(struct(nt * px, lev),) * 2,
        in_specs=[VMEM, VMEM, VMEM],
        out_specs=(VMEM, VMEM),
        scratch_shapes=[pltpu.VMEM((8 * px, lev), F32)],
        compiler_params=params(8),
        cost_estimate=cost(MIB, MIB),
        name="edges",
    )(edges, got_b, got_a)
    got_d = lax.ppermute(send_d, "blk", pair_d)
    got_c = lax.ppermute(send_c, "blk", pair_c)

    table, onehots, lanes, costs, first, second, bad = pl.pallas_call(
        gains_kernel,
        out_shape=(
            struct(groups, lev),
            struct(2 * groups, groups, dtype=BF16),
            struct(groups, lev),
            struct(groups, lev),
            struct(2 * lev, 2 * lev, dtype=BF16),
            struct(2 * lev, lev, dtype=BF16),
            struct(8, lev),
        ),
        in_specs=[VMEM] * 4,
        out_specs=(VMEM,) * 7,
        scratch_shapes=[pltpu.VMEM((MAXC, lev), F32)],
        compiler_params=params(8),
        cost_estimate=cost(512 * MIB, MIB),
        name="gains",
    )(mixing, destinations.reshape(1, groups), group_costs.reshape(1, groups), triggers)

    early = pl.pallas_call(
        early_rain_kernel,
        out_shape=struct(groups, lev),
        in_specs=[VMEM] * 4,
        out_specs=VMEM,
        scratch_shapes=[pltpu.VMEM((2, rows, lev), F32)],
        compiler_params=params(8),
        cost_estimate=cost(512 * MIB, MIB),
        name="early_rain",
    )(tracer, got_a, got_b, table)

    outgoing = pl.pallas_call(
        rain_kernel,
        out_shape=struct(groups, lev),
        in_specs=[VMEM] * 13,
        out_specs=VMEM,
        scratch_shapes=[pltpu.VMEM((groups, lev), F32), pltpu.VMEM((2, rows, lev), F32)],
        compiler_params=params(12),
        cost_estimate=cost(64 * MIB, 2 * MIB),
        name="rain",
    )(costs, bad, tracer, got_a, got_b, got_c, got_d, early, table, lanes, onehots, first, second)

    incoming = lax.all_to_all(outgoing, ("elem", "blk"), split_axis=0, concat_axis=0, tiled=True)

    chunks = 4
    new = pl.pallas_call(
        mix_kernel,
        out_shape=struct(px, rows, lev),
        in_specs=[HBM] * 11,
        out_specs=HBM,
        scratch_shapes=[
            pltpu.VMEM((px, rows, lev), F32),
            pltpu.VMEM((px, rows, lev), F32),
            pltpu.VMEM((MAXC, lev, 3 * lev), BF16),
            pltpu.SMEM((groups,), jnp.int32),
            pltpu.VMEM((8, lev), F32),
            pltpu.VMEM((lev, lev), F32),
            pltpu.VMEM((px, py), jnp.int32),
            pltpu.VMEM((rows, lev), F32),
            pltpu.VMEM((rows, lev), F32),
            pltpu.VMEM((nt * px, lev), F32),
            pltpu.VMEM((nt * px, lev), F32),
            pltpu.VMEM((2 * lev, 2 * lev), BF16),
            pltpu.VMEM((2 * lev, lev), BF16),
            pltpu.VMEM((rows, lev), F32),
            pltpu.SemaphoreType.DMA((chunks,)),
            pltpu.SemaphoreType.DMA((2 * chunks,)),
            pltpu.SemaphoreType.DMA((10,)),
        ],
        compiler_params=params(60),
        cost_estimate=cost(4096 * MIB, 10 * MIB),
        name="mix",
    )(group_costs, bad, mixing, triggers, got_a, got_b, got_c, got_d, first, second, kept(local))

    rain = pl.pallas_call(
        gather_kernel,
        out_shape=struct(groups * GROUP_COLS // lev, lev),
        in_specs=[VMEM],
        out_specs=VMEM,
        compiler_params=params(8),
        cost_estimate=cost(MIB, MIB),
        name="gather",
    )(incoming)
    return new.reshape(state.shape), rain.reshape(-1)


def solution(mesh):
    return jax.shard_map(
        body,
        mesh=mesh,
        in_specs=(
            P("elem", "blk", None, None),
            P("elem", "blk", None),
            P("elem", "blk", None),
            P(),
            P("elem", "blk"),
            P(("elem", "blk")),
            P(("elem", "blk")),
        ),
        out_specs=(P("elem", "blk", None, None), P(("elem", "blk"))),
        check_vma=False,
    )
```

```python
import functools

import jax
import jax.numpy as jnp
import numpy as np
from jax import lax
from jax.experimental import pallas as pl
from jax.experimental.pallas import tpu as pltpu
from jax.sharding import PartitionSpec as P

NP = 4
NT = 4
LEV = 128
GROUP_COLS = 16
MAXC = 64
LIMIT = 1.0e3
HUGE = 3.38e38
F32 = jnp.float32
BF16 = jnp.bfloat16
MIB = 1024 * 1024


def gll_derivative():
    nodes = np.array([-1.0, -1.0 / np.sqrt(5.0), 1.0 / np.sqrt(5.0), 1.0])
    legendre = (5.0 * nodes * nodes * nodes - 3.0 * nodes) / 2.0
    derivative = np.zeros((4, 4))
    for a in range(4):
        for b in range(4):
            if a != b:
                derivative[a, b] = legendre[a] / (legendre[b] * (nodes[a] - nodes[b]))
    derivative[0, 0] = -3.0
    derivative[3, 3] = 3.0
    return derivative


def split2(x):
    high = x.astype(BF16)
    return high, (x - high.astype(F32)).astype(BF16)


def split3(x):
    high = x.astype(BF16)
    rest = x - high.astype(F32)
    mid = rest.astype(BF16)
    return high, mid, (rest - mid.astype(F32)).astype(BF16)


def mm(a, b):
    return jnp.dot(a, b, preferred_element_type=F32)


def exact_pick(onehot, values):
    return mm(jnp.concatenate([onehot] * 3, axis=1), jnp.concatenate(split3(values), axis=0))


def weights(high, mid, low):
    pair = jnp.concatenate([high, mid], axis=1)
    return jnp.concatenate([pair, pair], axis=0), jnp.concatenate([low, high], axis=0)


def precise(high, mid, low, first, second):
    one = mm(jnp.concatenate([high, mid], axis=1), first)
    two = mm(jnp.concatenate([high, low], axis=1), second)
    return one[:, :LEV] + (one[:, LEV:] + two)


def repeated(start, cost, first_ref, second_ref):
    return lax.fori_loop(0, cost, lambda i, c: precise(*split3(c), first_ref[...], second_ref[...]), start)


def iota(shape, dim):
    return lax.broadcasted_iota(jnp.int32, shape, dim)


def gains_kernel(mixing_ref, dest_ref, cost_ref, trig_ref, table_ref, onehot_ref, lanes_ref, costs_ref, first_ref, second_ref, bad_ref, sums):
    square = mixing_ref[...]
    worst = jnp.max(jnp.abs(square))
    first_ref[...], second_ref[...] = weights(*split3(square.T))
    sums[0:8] = jnp.broadcast_to(jnp.sum(square, axis=0, keepdims=True), (8, LEV))
    for k in (1, 2, 4, 8, 16, 32):
        parts = split3(square)
        pair = weights(*parts)
        rows = max(k, 8)
        grown = precise(*split3(sums[0:rows]), *pair)
        if k < 8:
            pick = iota((8, LEV), 0)
            merged = sums[0:8]
            for j in range(k):
                merged = jnp.where(pick == j + k, grown[j:j + 1], merged)
            sums[0:8] = merged
        else:
            sums[k:2 * k] = grown
        if k < 32:
            square = precise(*parts, *pair)
            worst = jnp.maximum(worst, jnp.max(jnp.abs(square)))
    bad_ref[...] = jnp.full(bad_ref.shape, jnp.where(worst <= LIMIT, 0.0, 1.0), F32)

    px, py = trig_ref.shape
    half = py // 2
    groups = 2 * px
    shape = (groups, groups)
    first_at, second_at = iota(shape, 0), iota(shape, 1)
    number0 = 2 * (first_at % px) + first_at // px
    number1 = 2 * (second_at % px) + second_at // px
    diagonal = first_at == number1

    def across(row):
        return jnp.sum(jnp.where(first_at == second_at, row, 0), axis=1, keepdims=True)

    def ordered(row_ref):
        col = across(jnp.broadcast_to(row_ref[...], shape))
        return jnp.sum(jnp.where(diagonal, col, 0), axis=0, keepdims=True)

    dest_row = jnp.broadcast_to(ordered(dest_ref), shape)
    dest_col = across(dest_row)
    earlier = (dest_col == dest_row) & (number0 < number1)
    within = jnp.sum(jnp.where(earlier, 1, 0), axis=0, keepdims=True)
    at = dest_row == first_at
    onehot_ref[0:groups] = jnp.where(at & (within == 0), 1.0, 0.0).astype(BF16)
    onehot_ref[groups:2 * groups] = jnp.where(at & (within == 1), 1.0, 0.0).astype(BF16)

    cost_col = across(jnp.broadcast_to(ordered(cost_ref), shape))
    chosen = jnp.where(cost_col == iota((groups, MAXC), 1) + 1, 1.0, 0.0).astype(BF16)
    table_ref[...] = exact_pick(chosen, 1.0 - sums[...])
    costs_ref[...] = jnp.broadcast_to(cost_col, (groups, LEV)).astype(F32)

    wide = trig_ref[...].astype(F32).astype(BF16)
    lane = iota((py, LEV), 1)
    for h in range(2):
        placed = jnp.where((lane < 2 * half) & (lane % half + half * h == iota((py, LEV), 0)), 1.0, 0.0).astype(BF16)
        lanes_ref[h * px:h * px + px] = mm(wide, placed)


def half_coefs(first, second):
    return jnp.where(iota((8, LEV), 0) < 4, F32(first), F32(second))


def derivative_tables():
    deriv = -0.05 * gll_derivative()
    even = [float(np.float32(0.5 * (deriv[a, 0] + deriv[a, 3]))) for a in range(2)]
    odd = [[float(np.float32(0.5 * (deriv[a, b] - deriv[a, 3 - b]))) for b in range(2)] for a in range(2)]
    return even, odd


def tendency(k, points, load, load_x, load_y, store):
    even, odd = derivative_tables()
    c_even = half_coefs(even[0], -even[1])
    c_odd, c_cross = half_coefs(odd[0][0], odd[1][1]), half_coefs(odd[0][1], odd[1][0])
    lower = iota((8, LEV), 0) < 4
    v = [[load(a, 16 * k + 8 * h) for h in range(2)] for a in range(NP)]
    along_x = []
    for h in range(2):
        d0, d1 = v[0][h] - v[3][h], v[1][h] - v[2][h]
        mean = (v[0][h] + v[3][h]) - (v[1][h] + v[2][h])
        p0, p1 = even[0] * mean, even[1] * mean
        q0, q1 = odd[0][0] * d0 + odd[0][1] * d1, odd[1][0] * d0 + odd[1][1] * d1
        along_x.append((q0 + p0, q1 + p1, q1 - p1, q0 - p0))
    for a in points:
        r1 = pltpu.roll(v[a][1], 4, axis=0)
        add, sub = v[a][0] + r1, v[a][0] - r1
        odds = c_odd * sub + c_cross * pltpu.roll(sub, 4, axis=0)
        evens = c_even * (add - pltpu.roll(add, 4, axis=0))
        along_y = (odds + evens, pltpu.roll(odds - evens, 4, axis=0))
        for h in range(2):
            y = 4 * k + 2 * h
            wx = jnp.where(lower, load_x(a, y), load_x(a, y + 1))
            wy = jnp.where(lower, load_y(a, y), load_y(a, y + 1))
            store(a, 16 * k + 8 * h, wx * along_x[h][a] + wy * along_y[h])


def sides_kernel(state_hbm, wx_hbm, wy_hbm, send_b_ref, send_a_ref, state, wx, wy, ends, sems):
    even = lax.axis_index("elem") % 2 == 0
    px = state_hbm.shape[0]
    copies = []
    for i, (element, x) in enumerate(((0, 0), (px - NP, px - 1))):
        copies.append(
            [
                pltpu.make_async_copy(wx_hbm.at[x], wx.at[i], sems.at[2 + i]),
                pltpu.make_async_copy(wy_hbm.at[x], wy.at[i], sems.at[4 + i]),
                pltpu.make_async_copy(state_hbm.at[pl.ds(element, NP)], state.at[i], sems.at[i]),
            ]
        )
    for copy in copies[0] + copies[1]:
        copy.start()
    for s, at in ((0, 0), (1, NP - 1)):
        for copy in copies[s]:
            copy.wait()

        def load(a, i):
            return state[s, a, i:i + 8, :]

        def store(a, i, value):
            ends[s, i:i + 8, :] = value

        for k in range(state.shape[2] // 16):
            tendency(k, (at,), load, lambda a, y: wx[s, y:y + 1, :], lambda a, y: wy[s, y:y + 1, :], store)
    send_a_ref[...] = jnp.where(even, ends[1], ends[0])
    send_b_ref[...] = jnp.where(even, ends[0], ends[1])


def smooth_rows(v, up, down):
    m0, n0 = half_coefs(0.5, 1.0), half_coefs(0.5, 0.0)
    m1, n1 = half_coefs(1.0, 0.5), half_coefs(0.0, 0.5)
    r = [pltpu.roll(piece, 4, axis=0) for piece in v]
    out = []
    for i in range(len(v)):
        if i % 2 == 0:
            other = r[i - 1] if i else up
            out.append(m0 * v[i] if other is None else m0 * v[i] + n0 * other)
        else:
            other = r[i + 1] if i < len(v) - 1 else down
            out.append(m1 * v[i] if other is None else m1 * v[i] + n1 * other)
    return out


def local_kernel(state, wx, wy, adv_hbm, tracer_ref, edge_ref, tend, adv, sems):
    elements = state.shape[0] // NP
    rows = state.shape[1]
    lower = iota((8, LEV), 0) < 4

    def out_copy(e):
        piece = pl.ds(e * NP, NP)
        return pltpu.make_async_copy(adv.at[piece], adv_hbm.at[piece], sems.at[e])

    def differentiate(e):
        def load(a, i):
            return state[e * NP + a, i:i + 8, :]

        def store(a, i, value):
            tend[e * NP + a, i:i + 8, :] = value

        for k in range(rows // 16):
            tendency(k, range(NP), load, lambda a, y: wx[e * NP + a, y:y + 1, :], lambda a, y: wy[e * NP + a, y:y + 1, :], store)

    def finish(e):
        for a in range(NP):
            x = e * NP + a
            v = [tend[x, 8 * i:8 * i + 8, :] for i in range(rows // 8)]
            if a == 0:
                left = jnp.maximum(x - 1, 0)
                share = jnp.where(e > 0, 0.5, 0.0).astype(F32)
                v = [0.5 * v[i] + share * tend[left, 8 * i:8 * i + 8, :] for i in range(rows // 8)]
            if a == NP - 1:
                right = jnp.minimum(x + 1, elements * NP - 1)
                share = jnp.where(e < elements - 1, 0.5, 0.0).astype(F32)
                v = [0.5 * v[i] + share * tend[right, 8 * i:8 * i + 8, :] for i in range(rows // 8)]
            edge_ref[x] = jnp.where(lower, v[0], v[-1])
            for i, value in enumerate(smooth_rows(v, None, None)):
                adv[x, 8 * i:8 * i + 8, :] = state[x, 8 * i:8 * i + 8, :] + value
        out_copy(e).start()

    differentiate(0)

    def step(e, carry):
        differentiate(e)
        finish(e - 1)
        return carry

    lax.fori_loop(1, elements, step, 0)
    finish(elements - 1)
    for x in range(elements * NP):
        tracer_ref[x] = adv[x, pl.ds(1, rows // NT, stride=NT), :]
    for e in range(elements):
        out_copy(e).wait()


def edge_kernel(edge_ref, got_b_ref, got_a_ref, send_d_ref, send_c_ref, both):
    even = lax.axis_index("elem") % 2 == 0
    even_y = lax.axis_index("blk") % 2 == 0
    px = edge_ref.shape[0]
    rows = got_a_ref.shape[0]
    lower = iota((8, LEV), 0) < 4
    before = jnp.where(even, got_b_ref[...], got_a_ref[...])
    after = jnp.where(even, got_a_ref[...], got_b_ref[...])
    for x in range(px):
        both[8 * x:8 * x + 8, :] = edge_ref[x]
    for x, side in ((0, before), (px - 1, after)):
        both[8 * x:8 * x + 8, :] = edge_ref[x] + 0.5 * jnp.where(lower, side[0:8], side[rows - 8:rows])
    for t in range(NT):
        first = both[pl.ds(t, px, stride=8), :]
        final = both[pl.ds(NT + t, px, stride=8), :]
        send_c_ref[t * px:t * px + px, :] = jnp.where(even_y, final, first)
        send_d_ref[t * px:t * px + px, :] = jnp.where(even_y, first, final)


def side_shares(even, got_a_ref, got_b_ref, rows):
    before = [0.5 * jnp.where(even, got_b_ref[i:i + 8, :], got_a_ref[i:i + 8, :]) for i in range(0, rows, 8)]
    after = [0.5 * jnp.where(even, got_a_ref[i:i + 8, :], got_b_ref[i:i + 8, :]) for i in range(0, rows, 8)]
    return smooth_rows(before, None, None), smooth_rows(after, None, None)


def rain_place(half):
    lane = iota((half, LEV), 1)
    return (lane < 2 * half) & (lane % half == iota((half, LEV), 0))


def rain_row(part, place):
    sums = jnp.sum(part, axis=1, keepdims=True) * 0.125
    return jnp.sum(jnp.where(place, sums, 0.0), axis=0, keepdims=True)


def early_rain_kernel(tracer_ref, got_a_ref, got_b_ref, table_ref, rain_ref, side_ref):
    px, py, _ = tracer_ref.shape
    half = py // 2
    rows = py * NT
    for s, side in enumerate(side_shares(lax.axis_index("elem") % 2 == 0, got_a_ref, got_b_ref, rows)):
        for i, value in enumerate(side):
            side_ref[s, 8 * i:8 * i + 8, :] = value
    place = rain_place(half)

    def one(x, extra):
        for h in range(2):
            part = tracer_ref[x, half * h:half * h + half, :]
            if extra is not None:
                part = part + extra[half * h:half * h + half]
            at = pl.ds(h * px + x, 1)
            rain_ref[at, :] = rain_row(part * table_ref[at, :], place)

    for x in range(px):
        side = {0: 0, px - 1: 1}.get(x)
        one(x, None if side is None else side_ref[side, pl.ds(1, py, stride=NT), :])


def rain_kernel(costs_ref, bad_ref, tracer_ref, got_a_ref, got_b_ref, got_c_ref, got_d_ref, early_ref, table_ref, lanes_ref, onehot_ref, first_ref, second_ref, out_ref, rain_ref, side_ref):
    px, py, _ = tracer_ref.shape
    half = py // 2
    rows = py * NT
    groups = 2 * px
    even_y = lax.axis_index("blk") % 2 == 0
    up = 0.5 * jnp.where(even_y, got_d_ref[px:2 * px, :], got_c_ref[px:2 * px, :])
    down = 0.5 * jnp.where(even_y, got_c_ref[px:2 * px, :], got_d_ref[px:2 * px, :])

    lane = iota((groups, LEV), 1)

    def send(rain):
        rain = jnp.where(jnp.abs(rain) <= HUGE, rain, HUGE)
        values = jnp.where(lane >= 2 * half, 1.0, jnp.where(lanes_ref[...] > 0.5, rain, 0.0))
        picked = exact_pick(onehot_ref[...], values)
        first, second = picked[:groups], picked[groups:]
        out_ref[...] = jnp.where(lane < half, first, jnp.where(lane < 2 * half, second, first + second))

    sums = jnp.sum(jnp.concatenate([up, down], axis=0) * table_ref[...], axis=1, keepdims=True) * 0.125
    column = jnp.where(iota((groups, LEV), 0) < px, 0, half - 1)
    send(early_ref[...] + jnp.where((lane == column) | (lane == column + half), sums, 0.0))
    bad = jnp.max(bad_ref[...]) > 0.5

    @pl.when(bad)
    def _():
        for s, side in enumerate(side_shares(lax.axis_index("elem") % 2 == 0, got_a_ref, got_b_ref, rows)):
            for i, value in enumerate(side):
                side_ref[s, 8 * i:8 * i + 8, :] = value
        rain_ref[0:px, :] = up
        rain_ref[px:2 * px, :] = down
        place = rain_place(half)
        row = iota((half, LEV), 0)

        def one(x, carry):
            near = jnp.where(x == 0, 1.0, 0.0).astype(F32)
            far = jnp.where(x == px - 1, 1.0, 0.0).astype(F32)
            for h, at in ((0, 0), (1, half - 1)):
                def side(s):
                    return side_ref[s, pl.ds(1 + half * NT * h, half, stride=NT), :]

                here = pl.ds(h * px + x, 1)
                part = tracer_ref[x, half * h:half * h + half, :] + (near * side(0) + far * side(1))
                part = part + jnp.where(row == at, rain_ref[here, :], 0.0)
                done = repeated(part, jnp.max(costs_ref[here, :]).astype(jnp.int32), first_ref, second_ref)
                rain_ref[here, :] = rain_row(part - done, place)
            return carry

        lax.fori_loop(0, px, one, 0)
        send(rain_ref[...])


def mix_kernel(cost_hbm, bad_hbm, mixing_hbm, trig_hbm, got_a_hbm, got_b_hbm, got_c_hbm, got_d_hbm, first_hbm, second_hbm, adv_hbm, new_hbm, adv, new, powers, cost_ref, bad_ref, mixing_ref, trig_ref, got_a_ref, got_b_ref, got_c_ref, got_d_ref, first_ref, second_ref, mask_ref, sems, out_sems, small_sems):
    px, rows, _ = adv.shape
    py = rows // NT
    half = rows // 2
    chunks = sems.shape[0]
    size = px // chunks
    out = px // out_sems.shape[0]
    even_y = lax.axis_index("blk") % 2 == 0
    lower = iota((8, LEV), 0) < 4

    def in_copy(i):
        return pltpu.make_async_copy(adv_hbm.at[pl.ds(i * size, size)], adv.at[pl.ds(i * size, size)], sems.at[i])

    def out_copy(i):
        return pltpu.make_async_copy(new.at[pl.ds(i * out, out)], new_hbm.at[pl.ds(i * out, out)], out_sems.at[i])

    small = [
        pltpu.make_async_copy(src, dst, small_sems.at[i])
        for i, (src, dst) in enumerate(
            (
                (mixing_hbm, mixing_ref),
                (bad_hbm, bad_ref),
                (cost_hbm, cost_ref),
                (trig_hbm, trig_ref),
                (got_a_hbm, got_a_ref),
                (got_b_hbm, got_b_ref),
                (got_c_hbm, got_c_ref),
                (got_d_hbm, got_d_ref),
                (first_hbm, first_ref),
                (second_hbm, second_ref),
            )
        )
    ]
    for copy in small:
        copy.start()
    for i in range(chunks):
        in_copy(i).start()
    small[0].wait()
    small[1].wait()
    bad = jnp.max(bad_ref[...]) > 0.5
    good = jnp.logical_not(bad)

    @pl.when(good)
    def _():
        powers[0] = jnp.concatenate(split3(mixing_ref[...].T), axis=1)

        def part(j):
            return powers[j, :, 0:LEV], powers[j, :, LEV:2 * LEV], powers[j, :, 2 * LEV:3 * LEV]

        for k in (1, 2, 4, 8):
            first, second = weights(*part(k - 1))

            def step(j, carry):
                powers[j + k] = jnp.concatenate(split3(precise(*part(j), first, second)), axis=1)
                return carry

            lax.fori_loop(0, k, step, 0, unroll=True)

        for k in (16, 32):
            pair = powers[k - 1, :, 0:2 * LEV]
            both = jnp.concatenate([pair, pair], axis=0)

            def later(j, carry):
                value = mm(powers[j, :, 0:2 * LEV], both)
                powers[j + k, :, 0:2 * LEV] = jnp.concatenate(split2(value[:, :LEV] + value[:, LEV:]), axis=1)
                return carry

            lax.fori_loop(0, k, later, 0, unroll=8)

    for copy in small[2:]:
        copy.wait()
    trig = jnp.concatenate([trig_ref[...].astype(F32), jnp.zeros((LEV - px, py), F32)], axis=0).T
    spread = jnp.where(iota((rows, py), 0) // NT == iota((rows, py), 1), 1.0, 0.0).astype(BF16)
    mask_ref[...] = mm(spread, trig.astype(BF16))
    shares = side_shares(lax.axis_index("elem") % 2 == 0, got_a_ref, got_b_ref, rows)
    in_copy(0).wait()
    in_copy(chunks - 1).wait()
    for x, share in ((0, shares[0]), (px - 1, shares[1])):
        for i in range(rows // 8):
            adv[x, 8 * i:8 * i + 8, :] = adv[x, 8 * i:8 * i + 8, :] + share[i]

    def edged(x, h):
        start = adv[x, half * h:half * h + half, :]
        at = pl.ds(x, NT, stride=px)
        if h == 0:
            add = 0.5 * jnp.where(even_y, got_d_ref[at, :], got_c_ref[at, :])
            return jnp.concatenate([start[0:8] + jnp.where(lower, jnp.concatenate([add, add], axis=0), 0.0), start[8:]], axis=0)
        add = 0.5 * jnp.where(even_y, got_c_ref[at, :], got_d_ref[at, :])
        return jnp.concatenate([start[:half - 8], start[half - 8:] + jnp.where(lower, 0.0, jnp.concatenate([add, add], axis=0))], axis=0)

    def powered(x, h, start):
        high, low = split2(start)
        both = mm(jnp.concatenate([high, low], axis=0), powers[cost_ref[2 * x + h] - 1, :, 0:2 * LEV])
        return (both[:half, :LEV] + both[half:, :LEV]) + (both[:half, LEV:] + both[half:, LEV:])

    def step_by_step(x, h, start):
        return repeated(start, cost_ref[2 * x + h], first_ref, second_ref)

    def one(rule, x, mask):
        for h in range(2):
            start = edged(x, h)
            done = rule(x, h, start)
            new[x, half * h:half * h + half, :] = jnp.where(mask[half * h:half * h + half] > 0.5, done, start)

    def arrive(i):
        @pl.when((i > 0) & (i < chunks - 1))
        def _():
            in_copy(i).wait()

    @pl.when(good)
    def _():
        def chunk(i, carry):
            arrive(i)
            rolled = pltpu.roll(mask_ref[...], lax.rem(LEV - i * size, LEV), axis=1)
            for a in range(size):
                one(powered, i * size + a, jnp.broadcast_to(rolled[:, a:a + 1], (rows, LEV)))
                if a % out == out - 1:
                    out_copy(i * (size // out) + a // out).start()
            return carry

        lax.fori_loop(0, chunks, chunk, 0)

    @pl.when(bad)
    def _():
        def chunk(i, carry):
            arrive(i)

            def column(a, carry):
                x = i * size + a
                rolled = pltpu.roll(mask_ref[...], lax.rem(LEV - x, LEV), axis=1)
                one(step_by_step, x, jnp.broadcast_to(rolled[:, 0:1], (rows, LEV)))
                return carry

            lax.fori_loop(0, size, column, 0)
            for j in range(size // out):
                out_copy(i * (size // out) + j).start()
            return carry

        lax.fori_loop(0, chunks, chunk, 0)

    for i in range(px // out):
        out_copy(i).wait()


def gather_kernel(got_ref, rain_ref):
    got = got_ref[...]
    size = got.shape
    half = GROUP_COLS
    counts = jnp.where(iota(size, 1) < 2 * half, pltpu.roll(got, LEV // 2, axis=1), got)
    start = jnp.sum(jnp.where(iota(size, 0) < iota(size, 1), counts, 0.0), axis=0, keepdims=True).astype(jnp.int32)
    count = jnp.sum(jnp.where(iota(size, 0) == iota(size, 1), counts, 0.0), axis=0, keepdims=True).astype(jnp.int32)
    per = LEV // half
    rows = size[0] // per
    slot = (iota(size, 0) % rows) * per + iota(size, 0) // rows
    pick0 = jnp.where((slot == start) & (count > 0), 1.0, 0.0)
    pick1 = jnp.where((slot == start + 1) & (count > 1), 1.0, 0.0)
    picked = exact_pick(jnp.concatenate([pick0, pick1], axis=0).astype(BF16), got)
    lane = iota((rows, LEV), 1)
    first, second = picked[:size[0]], pltpu.roll(picked[size[0]:], LEV - half, axis=1)
    total = jnp.where(iota(size, 1) < half, first + second, 0.0)
    out = total[0:rows]
    for q in range(1, per):
        out = jnp.where(lane // half == q, pltpu.roll(total[q * rows:(q + 1) * rows], half * q, axis=1), out)
    rain_ref[...] = out


VMEM = pl.BlockSpec(memory_space=pltpu.VMEM)
HBM = pl.BlockSpec(memory_space=pltpu.HBM)


def params(mib):
    return pltpu.CompilerParams(vmem_limit_bytes=mib * MIB)


def cost(flops, moved):
    return pl.CostEstimate(flops=flops, bytes_accessed=moved, transcendentals=0)


def body(state, wind_x, wind_y, mixing, triggers, group_costs, destinations):
    px, py, nt, lev = state.shape
    rows = py * nt
    groups = group_costs.shape[0]
    elements = px // NP
    n_elem, n_blk = lax.axis_size("elem"), lax.axis_size("blk")
    slabs = state.reshape(px, rows, lev)
    def struct(*shape, dtype=F32):
        return jax.ShapeDtypeStruct(shape, dtype)

    def block(shape, *at):
        return pl.BlockSpec(shape, lambda i: at)

    def kept(x):
        return pltpu.with_memory_space_constraint(x, pltpu.HBM)

    send_b, send_a = pl.pallas_call(
        sides_kernel,
        out_shape=(struct(rows, lev),) * 2,
        in_specs=[HBM] * 3,
        out_specs=(VMEM, VMEM),
        scratch_shapes=[
            pltpu.VMEM((2, NP, rows, lev), F32),
            pltpu.VMEM((2, py, lev), F32),
            pltpu.VMEM((2, py, lev), F32),
            pltpu.VMEM((2, rows, lev), F32),
            pltpu.SemaphoreType.DMA((6,)),
        ],
        compiler_params=params(4),
        cost_estimate=cost(2 * MIB, MIB),
        name="sides",
    )(kept(slabs), kept(wind_x), kept(wind_y))

    pair_a = [(i, i ^ 1) for i in range(n_elem)]
    pair_b = [(i, (i - 1 if i % 2 == 0 else i + 1) % n_elem) for i in range(n_elem)]
    pair_c = [(j, j ^ 1) for j in range(n_blk)]
    pair_d = [(j, (j - 1 if j % 2 == 0 else j + 1) % n_blk) for j in range(n_blk)]
    got_b = lax.ppermute(send_b, "elem", pair_b)
    got_a = lax.ppermute(send_a, "elem", pair_a)

    local, tracer, edges = pl.pallas_call(
        local_kernel,
        out_shape=(pltpu.HBM((px, rows, lev), F32), struct(px, py, lev), struct(px, 8, lev)),
        in_specs=[VMEM, VMEM, VMEM],
        out_specs=(HBM, VMEM, VMEM),
        scratch_shapes=[
            pltpu.VMEM((px, rows, lev), F32),
            pltpu.VMEM((px, rows, lev), F32),
            pltpu.SemaphoreType.DMA((elements,)),
        ],
        compiler_params=params(14),
        cost_estimate=cost(64 * MIB, 12 * MIB),
        name="local",
    )(slabs, wind_x, wind_y)

    send_d, send_c = pl.pallas_call(
        edge_kernel,
        out_shape=(struct(nt * px, lev),) * 2,
        in_specs=[VMEM, VMEM, VMEM],
        out_specs=(VMEM, VMEM),
        scratch_shapes=[pltpu.VMEM((8 * px, lev), F32)],
        compiler_params=params(8),
        cost_estimate=cost(MIB, MIB),
        name="edges",
    )(edges, got_b, got_a)
    got_d = lax.ppermute(send_d, "blk", pair_d)
    got_c = lax.ppermute(send_c, "blk", pair_c)

    table, onehots, lanes, costs, first, second, bad = pl.pallas_call(
        gains_kernel,
        out_shape=(
            struct(groups, lev),
            struct(2 * groups, groups, dtype=BF16),
            struct(groups, lev),
            struct(groups, lev),
            struct(2 * lev, 2 * lev, dtype=BF16),
            struct(2 * lev, lev, dtype=BF16),
            struct(8, lev),
        ),
        in_specs=[VMEM] * 4,
        out_specs=(VMEM,) * 7,
        scratch_shapes=[pltpu.VMEM((MAXC, lev), F32)],
        compiler_params=params(8),
        cost_estimate=cost(512 * MIB, MIB),
        name="gains",
    )(mixing, destinations.reshape(1, groups), group_costs.reshape(1, groups), triggers)

    early = pl.pallas_call(
        early_rain_kernel,
        out_shape=struct(groups, lev),
        in_specs=[VMEM] * 4,
        out_specs=VMEM,
        scratch_shapes=[pltpu.VMEM((2, rows, lev), F32)],
        compiler_params=params(8),
        cost_estimate=cost(512 * MIB, MIB),
        name="early_rain",
    )(tracer, got_a, got_b, table)

    outgoing = pl.pallas_call(
        rain_kernel,
        out_shape=struct(groups, lev),
        in_specs=[VMEM] * 13,
        out_specs=VMEM,
        scratch_shapes=[pltpu.VMEM((groups, lev), F32), pltpu.VMEM((2, rows, lev), F32)],
        compiler_params=params(12),
        cost_estimate=cost(64 * MIB, 2 * MIB),
        name="rain",
    )(costs, bad, tracer, got_a, got_b, got_c, got_d, early, table, lanes, onehots, first, second)

    incoming = lax.all_to_all(outgoing, ("elem", "blk"), split_axis=0, concat_axis=0, tiled=True)

    chunks = 4
    new = pl.pallas_call(
        mix_kernel,
        out_shape=struct(px, rows, lev),
        in_specs=[HBM] * 11,
        out_specs=HBM,
        scratch_shapes=[
            pltpu.VMEM((px, rows, lev), F32),
            pltpu.VMEM((px, rows, lev), F32),
            pltpu.VMEM((MAXC, lev, 3 * lev), BF16),
            pltpu.SMEM((groups,), jnp.int32),
            pltpu.VMEM((8, lev), F32),
            pltpu.VMEM((lev, lev), F32),
            pltpu.VMEM((px, py), jnp.int32),
            pltpu.VMEM((rows, lev), F32),
            pltpu.VMEM((rows, lev), F32),
            pltpu.VMEM((nt * px, lev), F32),
            pltpu.VMEM((nt * px, lev), F32),
            pltpu.VMEM((2 * lev, 2 * lev), BF16),
            pltpu.VMEM((2 * lev, lev), BF16),
            pltpu.VMEM((rows, lev), F32),
            pltpu.SemaphoreType.DMA((chunks,)),
            pltpu.SemaphoreType.DMA((2 * chunks,)),
            pltpu.SemaphoreType.DMA((10,)),
        ],
        compiler_params=params(60),
        cost_estimate=cost(4096 * MIB, 10 * MIB),
        name="mix",
    )(group_costs, bad, mixing, triggers, got_a, got_b, got_c, got_d, first, second, kept(local))

    rain = pl.pallas_call(
        gather_kernel,
        out_shape=struct(groups * GROUP_COLS // lev, lev),
        in_specs=[VMEM],
        out_specs=VMEM,
        compiler_params=params(8),
        cost_estimate=cost(MIB, MIB),
        name="gather",
    )(incoming)
    return new.reshape(state.shape), rain.reshape(-1)


def solution(mesh):
    return jax.shard_map(
        body,
        mesh=mesh,
        in_specs=(
            P("elem", "blk", None, None),
            P("elem", "blk", None),
            P("elem", "blk", None),
            P(),
            P("elem", "blk"),
            P(("elem", "blk")),
            P(("elem", "blk")),
        ),
        out_specs=(P("elem", "blk", None, None), P(("elem", "blk"))),
        check_vma=False,
    )
```

```python
import functools

import jax
import jax.numpy as jnp
import numpy as np
from jax import lax
from jax.experimental import pallas as pl
from jax.experimental.pallas import tpu as pltpu
from jax.sharding import PartitionSpec as P

NP = 4
NT = 4
LEV = 128
GROUP_COLS = 16
MAXC = 64
LIMIT = 1.0e3
HUGE = 3.38e38
F32 = jnp.float32
BF16 = jnp.bfloat16
MIB = 1024 * 1024


def gll_derivative():
    nodes = np.array([-1.0, -1.0 / np.sqrt(5.0), 1.0 / np.sqrt(5.0), 1.0])
    legendre = (5.0 * nodes * nodes * nodes - 3.0 * nodes) / 2.0
    derivative = np.zeros((4, 4))
    for a in range(4):
        for b in range(4):
            if a != b:
                derivative[a, b] = legendre[a] / (legendre[b] * (nodes[a] - nodes[b]))
    derivative[0, 0] = -3.0
    derivative[3, 3] = 3.0
    return derivative


def split2(x):
    high = x.astype(BF16)
    return high, (x - high.astype(F32)).astype(BF16)


def split3(x):
    high = x.astype(BF16)
    rest = x - high.astype(F32)
    mid = rest.astype(BF16)
    return high, mid, (rest - mid.astype(F32)).astype(BF16)


def mm(a, b):
    return jnp.dot(a, b, preferred_element_type=F32)


def exact_pick(onehot, values):
    return mm(jnp.concatenate([onehot] * 3, axis=1), jnp.concatenate(split3(values), axis=0))


def weights(high, mid, low):
    pair = jnp.concatenate([high, mid], axis=1)
    return jnp.concatenate([pair, pair], axis=0), jnp.concatenate([low, high], axis=0)


def precise(high, mid, low, first, second):
    one = mm(jnp.concatenate([high, mid], axis=1), first)
    two = mm(jnp.concatenate([high, low], axis=1), second)
    return one[:, :LEV] + (one[:, LEV:] + two)


def repeated(start, cost, first_ref, second_ref):
    return lax.fori_loop(0, cost, lambda i, c: precise(*split3(c), first_ref[...], second_ref[...]), start)


def iota(shape, dim):
    return lax.broadcasted_iota(jnp.int32, shape, dim)


def gains_kernel(mixing_ref, dest_ref, cost_ref, trig_ref, table_ref, onehot_ref, lanes_ref, costs_ref, first_ref, second_ref, bad_ref, sums):
    square = mixing_ref[...]
    worst = jnp.max(jnp.abs(square))
    first_ref[...], second_ref[...] = weights(*split3(square.T))
    sums[0:8] = jnp.broadcast_to(jnp.sum(square, axis=0, keepdims=True), (8, LEV))
    for k in (1, 2, 4, 8, 16, 32):
        parts = split3(square)
        pair = weights(*parts)
        rows = max(k, 8)
        grown = precise(*split3(sums[0:rows]), *pair)
        if k < 8:
            pick = iota((8, LEV), 0)
            merged = sums[0:8]
            for j in range(k):
                merged = jnp.where(pick == j + k, grown[j:j + 1], merged)
            sums[0:8] = merged
        else:
            sums[k:2 * k] = grown
        if k < 32:
            square = precise(*parts, *pair)
            worst = jnp.maximum(worst, jnp.max(jnp.abs(square)))
    bad_ref[...] = jnp.full(bad_ref.shape, jnp.where(worst <= LIMIT, 0.0, 1.0), F32)

    px, py = trig_ref.shape
    half = py // 2
    groups = 2 * px
    shape = (groups, groups)
    first_at, second_at = iota(shape, 0), iota(shape, 1)
    number0 = 2 * (first_at % px) + first_at // px
    number1 = 2 * (second_at % px) + second_at // px
    diagonal = first_at == number1

    def across(row):
        return jnp.sum(jnp.where(first_at == second_at, row, 0), axis=1, keepdims=True)

    def ordered(row_ref):
        col = across(jnp.broadcast_to(row_ref[...], shape))
        return jnp.sum(jnp.where(diagonal, col, 0), axis=0, keepdims=True)

    dest_row = jnp.broadcast_to(ordered(dest_ref), shape)
    dest_col = across(dest_row)
    earlier = (dest_col == dest_row) & (number0 < number1)
    within = jnp.sum(jnp.where(earlier, 1, 0), axis=0, keepdims=True)
    at = dest_row == first_at
    onehot_ref[0:groups] = jnp.where(at & (within == 0), 1.0, 0.0).astype(BF16)
    onehot_ref[groups:2 * groups] = jnp.where(at & (within == 1), 1.0, 0.0).astype(BF16)

    cost_col = across(jnp.broadcast_to(ordered(cost_ref), shape))
    chosen = jnp.where(cost_col == iota((groups, MAXC), 1) + 1, 1.0, 0.0).astype(BF16)
    table_ref[...] = exact_pick(chosen, 1.0 - sums[...])
    costs_ref[...] = jnp.broadcast_to(cost_col, (groups, LEV)).astype(F32)

    wide = trig_ref[...].astype(F32).astype(BF16)
    lane = iota((py, LEV), 1)
    for h in range(2):
        placed = jnp.where((lane < 2 * half) & (lane % half + half * h == iota((py, LEV), 0)), 1.0, 0.0).astype(BF16)
        lanes_ref[h * px:h * px + px] = mm(wide, placed)


def half_coefs(first, second):
    return jnp.where(iota((8, LEV), 0) < 4, F32(first), F32(second))


def derivative_tables():
    deriv = -0.05 * gll_derivative()
    even = [float(np.float32(0.5 * (deriv[a, 0] + deriv[a, 3]))) for a in range(2)]
    odd = [[float(np.float32(0.5 * (deriv[a, b] - deriv[a, 3 - b]))) for b in range(2)] for a in range(2)]
    return even, odd


def tendency(k, points, load, load_x, load_y, store):
    even, odd = derivative_tables()
    c_even = half_coefs(even[0], -even[1])
    c_odd, c_cross = half_coefs(odd[0][0], odd[1][1]), half_coefs(odd[0][1], odd[1][0])
    lower = iota((8, LEV), 0) < 4
    v = [[load(a, 16 * k + 8 * h) for h in range(2)] for a in range(NP)]
    along_x = []
    for h in range(2):
        d0, d1 = v[0][h] - v[3][h], v[1][h] - v[2][h]
        mean = (v[0][h] + v[3][h]) - (v[1][h] + v[2][h])
        p0, p1 = even[0] * mean, even[1] * mean
        q0, q1 = odd[0][0] * d0 + odd[0][1] * d1, odd[1][0] * d0 + odd[1][1] * d1
        along_x.append((q0 + p0, q1 + p1, q1 - p1, q0 - p0))
    for a in points:
        r1 = pltpu.roll(v[a][1], 4, axis=0)
        add, sub = v[a][0] + r1, v[a][0] - r1
        odds = c_odd * sub + c_cross * pltpu.roll(sub, 4, axis=0)
        evens = c_even * (add - pltpu.roll(add, 4, axis=0))
        along_y = (odds + evens, pltpu.roll(odds - evens, 4, axis=0))
        for h in range(2):
            y = 4 * k + 2 * h
            wx = jnp.where(lower, load_x(a, y), load_x(a, y + 1))
            wy = jnp.where(lower, load_y(a, y), load_y(a, y + 1))
            store(a, 16 * k + 8 * h, wx * along_x[h][a] + wy * along_y[h])


def sides_kernel(state_hbm, wx_hbm, wy_hbm, send_b_ref, send_a_ref, state, wx, wy, ends, sems):
    even = lax.axis_index("elem") % 2 == 0
    px = state_hbm.shape[0]
    copies = []
    for i, (element, x) in enumerate(((0, 0), (px - NP, px - 1))):
        copies.append(
            [
                pltpu.make_async_copy(wx_hbm.at[x], wx.at[i], sems.at[2 + i]),
                pltpu.make_async_copy(wy_hbm.at[x], wy.at[i], sems.at[4 + i]),
            ]
            + [pltpu.make_async_copy(state_hbm.at[element + a], state.at[i, a], sems.at[6 + NP * i + a]) for a in range(NP)]
        )
    for copy in copies[0] + copies[1]:
        copy.start(priority=1)
    for s, at in ((0, 0), (1, NP - 1)):
        for copy in copies[s]:
            copy.wait()

        def load(a, i):
            return state[s, a, i:i + 8, :]

        def store(a, i, value):
            ends[s, i:i + 8, :] = value

        for k in range(state.shape[2] // 16):
            tendency(k, (at,), load, lambda a, y: wx[s, y:y + 1, :], lambda a, y: wy[s, y:y + 1, :], store)
    send_a_ref[...] = jnp.where(even, ends[1], ends[0])
    send_b_ref[...] = jnp.where(even, ends[0], ends[1])


def smooth_rows(v, up, down):
    m0, n0 = half_coefs(0.5, 1.0), half_coefs(0.5, 0.0)
    m1, n1 = half_coefs(1.0, 0.5), half_coefs(0.0, 0.5)
    r = [pltpu.roll(piece, 4, axis=0) for piece in v]
    out = []
    for i in range(len(v)):
        if i % 2 == 0:
            other = r[i - 1] if i else up
            out.append(m0 * v[i] if other is None else m0 * v[i] + n0 * other)
        else:
            other = r[i + 1] if i < len(v) - 1 else down
            out.append(m1 * v[i] if other is None else m1 * v[i] + n1 * other)
    return out


def local_kernel(state, wx, wy, adv_hbm, tracer_ref, edge_ref, tend, adv, sems):
    elements = state.shape[0] // NP
    rows = state.shape[1]
    lower = iota((8, LEV), 0) < 4

    def out_copy(e):
        piece = pl.ds(e * NP, NP)
        return pltpu.make_async_copy(adv.at[piece], adv_hbm.at[piece], sems.at[e])

    def differentiate(e):
        def load(a, i):
            return state[e * NP + a, i:i + 8, :]

        def store(a, i, value):
            tend[e * NP + a, i:i + 8, :] = value

        for k in range(rows // 16):
            tendency(k, range(NP), load, lambda a, y: wx[e * NP + a, y:y + 1, :], lambda a, y: wy[e * NP + a, y:y + 1, :], store)

    def finish(e):
        for a in range(NP):
            x = e * NP + a
            v = [tend[x, 8 * i:8 * i + 8, :] for i in range(rows // 8)]
            if a == 0:
                left = jnp.maximum(x - 1, 0)
                share = jnp.where(e > 0, 0.5, 0.0).astype(F32)
                v = [0.5 * v[i] + share * tend[left, 8 * i:8 * i + 8, :] for i in range(rows // 8)]
            if a == NP - 1:
                right = jnp.minimum(x + 1, elements * NP - 1)
                share = jnp.where(e < elements - 1, 0.5, 0.0).astype(F32)
                v = [0.5 * v[i] + share * tend[right, 8 * i:8 * i + 8, :] for i in range(rows // 8)]
            edge_ref[x] = jnp.where(lower, v[0], v[-1])
            for i, value in enumerate(smooth_rows(v, None, None)):
                adv[x, 8 * i:8 * i + 8, :] = state[x, 8 * i:8 * i + 8, :] + value
        out_copy(e).start()

    differentiate(0)

    def step(e, carry):
        differentiate(e)
        finish(e - 1)
        return carry

    lax.fori_loop(1, elements, step, 0)
    finish(elements - 1)
    for x in range(elements * NP):
        tracer_ref[x] = adv[x, pl.ds(1, rows // NT, stride=NT), :]
    for e in range(elements):
        out_copy(e).wait()


def edge_kernel(edge_ref, got_b_ref, got_a_ref, send_d_ref, send_c_ref, both):
    even = lax.axis_index("elem") % 2 == 0
    even_y = lax.axis_index("blk") % 2 == 0
    px = edge_ref.shape[0]
    rows = got_a_ref.shape[0]
    lower = iota((8, LEV), 0) < 4
    before = jnp.where(even, got_b_ref[...], got_a_ref[...])
    after = jnp.where(even, got_a_ref[...], got_b_ref[...])
    for x in range(px):
        both[8 * x:8 * x + 8, :] = edge_ref[x]
    for x, side in ((0, before), (px - 1, after)):
        both[8 * x:8 * x + 8, :] = edge_ref[x] + 0.5 * jnp.where(lower, side[0:8], side[rows - 8:rows])
    for t in range(NT):
        first = both[pl.ds(t, px, stride=8), :]
        final = both[pl.ds(NT + t, px, stride=8), :]
        send_c_ref[t * px:t * px + px, :] = jnp.where(even_y, final, first)
        send_d_ref[t * px:t * px + px, :] = jnp.where(even_y, first, final)


def side_shares(even, got_a_ref, got_b_ref, rows):
    before = [0.5 * jnp.where(even, got_b_ref[i:i + 8, :], got_a_ref[i:i + 8, :]) for i in range(0, rows, 8)]
    after = [0.5 * jnp.where(even, got_a_ref[i:i + 8, :], got_b_ref[i:i + 8, :]) for i in range(0, rows, 8)]
    return smooth_rows(before, None, None), smooth_rows(after, None, None)


def rain_place(half):
    lane = iota((half, LEV), 1)
    return (lane < 2 * half) & (lane % half == iota((half, LEV), 0))


def rain_row(part, place):
    sums = jnp.sum(part, axis=1, keepdims=True) * 0.125
    return jnp.sum(jnp.where(place, sums, 0.0), axis=0, keepdims=True)


def early_rain_kernel(tracer_ref, got_a_ref, got_b_ref, table_ref, rain_ref, side_ref):
    px, py, _ = tracer_ref.shape
    half = py // 2
    rows = py * NT
    for s, side in enumerate(side_shares(lax.axis_index("elem") % 2 == 0, got_a_ref, got_b_ref, rows)):
        for i, value in enumerate(side):
            side_ref[s, 8 * i:8 * i + 8, :] = value
    place = rain_place(half)

    def one(x, extra):
        for h in range(2):
            part = tracer_ref[x, half * h:half * h + half, :]
            if extra is not None:
                part = part + extra[half * h:half * h + half]
            at = pl.ds(h * px + x, 1)
            rain_ref[at, :] = rain_row(part * table_ref[at, :], place)

    for x in range(px):
        side = {0: 0, px - 1: 1}.get(x)
        one(x, None if side is None else side_ref[side, pl.ds(1, py, stride=NT), :])


def rain_kernel(costs_ref, bad_ref, tracer_ref, got_a_ref, got_b_ref, got_c_ref, got_d_ref, early_ref, table_ref, lanes_ref, onehot_ref, first_ref, second_ref, out_ref, rain_ref, side_ref):
    px, py, _ = tracer_ref.shape
    half = py // 2
    rows = py * NT
    groups = 2 * px
    even_y = lax.axis_index("blk") % 2 == 0
    up = 0.5 * jnp.where(even_y, got_d_ref[px:2 * px, :], got_c_ref[px:2 * px, :])
    down = 0.5 * jnp.where(even_y, got_c_ref[px:2 * px, :], got_d_ref[px:2 * px, :])

    lane = iota((groups, LEV), 1)

    def send(rain):
        rain = jnp.where(jnp.abs(rain) <= HUGE, rain, HUGE)
        values = jnp.where(lane >= 2 * half, 1.0, jnp.where(lanes_ref[...] > 0.5, rain, 0.0))
        picked = exact_pick(onehot_ref[...], values)
        first, second = picked[:groups], picked[groups:]
        out_ref[...] = jnp.where(lane < half, first, jnp.where(lane < 2 * half, second, first + second))

    sums = jnp.sum(jnp.concatenate([up, down], axis=0) * table_ref[...], axis=1, keepdims=True) * 0.125
    column = jnp.where(iota((groups, LEV), 0) < px, 0, half - 1)
    send(early_ref[...] + jnp.where((lane == column) | (lane == column + half), sums, 0.0))
    bad = jnp.max(bad_ref[...]) > 0.5

    @pl.when(bad)
    def _():
        for s, side in enumerate(side_shares(lax.axis_index("elem") % 2 == 0, got_a_ref, got_b_ref, rows)):
            for i, value in enumerate(side):
                side_ref[s, 8 * i:8 * i + 8, :] = value
        rain_ref[0:px, :] = up
        rain_ref[px:2 * px, :] = down
        place = rain_place(half)
        row = iota((half, LEV), 0)

        def one(x, carry):
            near = jnp.where(x == 0, 1.0, 0.0).astype(F32)
            far = jnp.where(x == px - 1, 1.0, 0.0).astype(F32)
            for h, at in ((0, 0), (1, half - 1)):
                def side(s):
                    return side_ref[s, pl.ds(1 + half * NT * h, half, stride=NT), :]

                here = pl.ds(h * px + x, 1)
                part = tracer_ref[x, half * h:half * h + half, :] + (near * side(0) + far * side(1))
                part = part + jnp.where(row == at, rain_ref[here, :], 0.0)
                done = repeated(part, jnp.max(costs_ref[here, :]).astype(jnp.int32), first_ref, second_ref)
                rain_ref[here, :] = rain_row(part - done, place)
            return carry

        lax.fori_loop(0, px, one, 0)
        send(rain_ref[...])


def mix_kernel(cost_hbm, bad_hbm, mixing_hbm, trig_hbm, got_a_hbm, got_b_hbm, got_c_hbm, got_d_hbm, first_hbm, second_hbm, adv_hbm, new_hbm, adv, new, powers, cost_ref, bad_ref, mixing_ref, trig_ref, got_a_ref, got_b_ref, got_c_ref, got_d_ref, first_ref, second_ref, mask_ref, sems, out_sems, small_sems):
    px, rows, _ = adv.shape
    py = rows // NT
    half = rows // 2
    chunks = sems.shape[0]
    size = px // chunks
    out = px // out_sems.shape[0]
    even_y = lax.axis_index("blk") % 2 == 0
    lower = iota((8, LEV), 0) < 4

    def in_copy(i):
        return pltpu.make_async_copy(adv_hbm.at[pl.ds(i * size, size)], adv.at[pl.ds(i * size, size)], sems.at[i])

    def out_copy(i):
        return pltpu.make_async_copy(new.at[pl.ds(i * out, out)], new_hbm.at[pl.ds(i * out, out)], out_sems.at[i])

    small = [
        pltpu.make_async_copy(src, dst, small_sems.at[i])
        for i, (src, dst) in enumerate(
            (
                (mixing_hbm, mixing_ref),
                (bad_hbm, bad_ref),
                (cost_hbm, cost_ref),
                (trig_hbm, trig_ref),
                (got_a_hbm, got_a_ref),
                (got_b_hbm, got_b_ref),
                (got_c_hbm, got_c_ref),
                (got_d_hbm, got_d_ref),
                (first_hbm, first_ref),
                (second_hbm, second_ref),
            )
        )
    ]
    for copy in small:
        copy.start()
    for i in range(chunks):
        in_copy(i).start()
    small[0].wait()
    small[1].wait()
    bad = jnp.max(bad_ref[...]) > 0.5
    good = jnp.logical_not(bad)

    @pl.when(good)
    def _():
        powers[0] = jnp.concatenate(split3(mixing_ref[...].T), axis=1)

        def part(j):
            return powers[j, :, 0:LEV], powers[j, :, LEV:2 * LEV], powers[j, :, 2 * LEV:3 * LEV]

        for k in (1, 2, 4, 8):
            first, second = weights(*part(k - 1))

            def step(j, carry):
                powers[j + k] = jnp.concatenate(split3(precise(*part(j), first, second)), axis=1)
                return carry

            lax.fori_loop(0, k, step, 0, unroll=True)

        for k in (16, 32):
            pair = powers[k - 1, :, 0:2 * LEV]
            both = jnp.concatenate([pair, pair], axis=0)

            def later(j, carry):
                value = mm(powers[j, :, 0:2 * LEV], both)
                powers[j + k, :, 0:2 * LEV] = jnp.concatenate(split2(value[:, :LEV] + value[:, LEV:]), axis=1)
                return carry

            lax.fori_loop(0, k, later, 0, unroll=8)

    for copy in small[2:]:
        copy.wait()
    trig = jnp.concatenate([trig_ref[...].astype(F32), jnp.zeros((LEV - px, py), F32)], axis=0).T
    spread = jnp.where(iota((rows, py), 0) // NT == iota((rows, py), 1), 1.0, 0.0).astype(BF16)
    mask_ref[...] = mm(spread, trig.astype(BF16))
    shares = side_shares(lax.axis_index("elem") % 2 == 0, got_a_ref, got_b_ref, rows)
    in_copy(0).wait()
    in_copy(chunks - 1).wait()
    for x, share in ((0, shares[0]), (px - 1, shares[1])):
        for i in range(rows // 8):
            adv[x, 8 * i:8 * i + 8, :] = adv[x, 8 * i:8 * i + 8, :] + share[i]

    def edged(x, h):
        start = adv[x, half * h:half * h + half, :]
        at = pl.ds(x, NT, stride=px)
        if h == 0:
            add = 0.5 * jnp.where(even_y, got_d_ref[at, :], got_c_ref[at, :])
            return jnp.concatenate([start[0:8] + jnp.where(lower, jnp.concatenate([add, add], axis=0), 0.0), start[8:]], axis=0)
        add = 0.5 * jnp.where(even_y, got_c_ref[at, :], got_d_ref[at, :])
        return jnp.concatenate([start[:half - 8], start[half - 8:] + jnp.where(lower, 0.0, jnp.concatenate([add, add], axis=0))], axis=0)

    def powered(x, h, start):
        high, low = split2(start)
        both = mm(jnp.concatenate([high, low], axis=0), powers[cost_ref[2 * x + h] - 1, :, 0:2 * LEV])
        return (both[:half, :LEV] + both[half:, :LEV]) + (both[:half, LEV:] + both[half:, LEV:])

    def step_by_step(x, h, start):
        return repeated(start, cost_ref[2 * x + h], first_ref, second_ref)

    def one(rule, x, mask):
        for h in range(2):
            start = edged(x, h)
            done = rule(x, h, start)
            new[x, half * h:half * h + half, :] = jnp.where(mask[half * h:half * h + half] > 0.5, done, start)

    def arrive(i):
        @pl.when((i > 0) & (i < chunks - 1))
        def _():
            in_copy(i).wait()

    @pl.when(good)
    def _():
        def chunk(i, carry):
            arrive(i)
            rolled = pltpu.roll(mask_ref[...], lax.rem(LEV - i * size, LEV), axis=1)
            for a in range(size):
                one(powered, i * size + a, jnp.broadcast_to(rolled[:, a:a + 1], (rows, LEV)))
                if a % out == out - 1:
                    out_copy(i * (size // out) + a // out).start()
            return carry

        lax.fori_loop(0, chunks, chunk, 0)

    @pl.when(bad)
    def _():
        def chunk(i, carry):
            arrive(i)

            def column(a, carry):
                x = i * size + a
                rolled = pltpu.roll(mask_ref[...], lax.rem(LEV - x, LEV), axis=1)
                one(step_by_step, x, jnp.broadcast_to(rolled[:, 0:1], (rows, LEV)))
                return carry

            lax.fori_loop(0, size, column, 0)
            for j in range(size // out):
                out_copy(i * (size // out) + j).start()
            return carry

        lax.fori_loop(0, chunks, chunk, 0)

    for i in range(px // out):
        out_copy(i).wait()


def gather_kernel(got_ref, rain_ref):
    got = got_ref[...]
    size = got.shape
    half = GROUP_COLS
    counts = jnp.where(iota(size, 1) < 2 * half, pltpu.roll(got, LEV // 2, axis=1), got)
    start = jnp.sum(jnp.where(iota(size, 0) < iota(size, 1), counts, 0.0), axis=0, keepdims=True).astype(jnp.int32)
    count = jnp.sum(jnp.where(iota(size, 0) == iota(size, 1), counts, 0.0), axis=0, keepdims=True).astype(jnp.int32)
    per = LEV // half
    rows = size[0] // per
    slot = (iota(size, 0) % rows) * per + iota(size, 0) // rows
    pick0 = jnp.where((slot == start) & (count > 0), 1.0, 0.0)
    pick1 = jnp.where((slot == start + 1) & (count > 1), 1.0, 0.0)
    picked = exact_pick(jnp.concatenate([pick0, pick1], axis=0).astype(BF16), got)
    lane = iota((rows, LEV), 1)
    first, second = picked[:size[0]], pltpu.roll(picked[size[0]:], LEV - half, axis=1)
    total = jnp.where(iota(size, 1) < half, first + second, 0.0)
    out = total[0:rows]
    for q in range(1, per):
        out = jnp.where(lane // half == q, pltpu.roll(total[q * rows:(q + 1) * rows], half * q, axis=1), out)
    rain_ref[...] = out


VMEM = pl.BlockSpec(memory_space=pltpu.VMEM)
HBM = pl.BlockSpec(memory_space=pltpu.HBM)


def params(mib):
    return pltpu.CompilerParams(vmem_limit_bytes=mib * MIB)


def cost(flops, moved):
    return pl.CostEstimate(flops=flops, bytes_accessed=moved, transcendentals=0)


def body(state, wind_x, wind_y, mixing, triggers, group_costs, destinations):
    px, py, nt, lev = state.shape
    rows = py * nt
    groups = group_costs.shape[0]
    elements = px // NP
    n_elem, n_blk = lax.axis_size("elem"), lax.axis_size("blk")
    slabs = state.reshape(px, rows, lev)
    def struct(*shape, dtype=F32):
        return jax.ShapeDtypeStruct(shape, dtype)

    def block(shape, *at):
        return pl.BlockSpec(shape, lambda i: at)

    def kept(x):
        return pltpu.with_memory_space_constraint(x, pltpu.HBM)

    send_b, send_a = pl.pallas_call(
        sides_kernel,
        out_shape=(struct(rows, lev),) * 2,
        in_specs=[HBM] * 3,
        out_specs=(VMEM, VMEM),
        scratch_shapes=[
            pltpu.VMEM((2, NP, rows, lev), F32),
            pltpu.VMEM((2, py, lev), F32),
            pltpu.VMEM((2, py, lev), F32),
            pltpu.VMEM((2, rows, lev), F32),
            pltpu.SemaphoreType.DMA((6 + 2 * NP,)),
        ],
        compiler_params=params(4),
        cost_estimate=cost(2 * MIB, MIB),
        name="sides",
    )(kept(slabs), kept(wind_x), kept(wind_y))

    pair_a = [(i, i ^ 1) for i in range(n_elem)]
    pair_b = [(i, (i - 1 if i % 2 == 0 else i + 1) % n_elem) for i in range(n_elem)]
    pair_c = [(j, j ^ 1) for j in range(n_blk)]
    pair_d = [(j, (j - 1 if j % 2 == 0 else j + 1) % n_blk) for j in range(n_blk)]
    got_b = lax.ppermute(send_b, "elem", pair_b)
    got_a = lax.ppermute(send_a, "elem", pair_a)

    local, tracer, edges = pl.pallas_call(
        local_kernel,
        out_shape=(pltpu.HBM((px, rows, lev), F32), struct(px, py, lev), struct(px, 8, lev)),
        in_specs=[VMEM, VMEM, VMEM],
        out_specs=(HBM, VMEM, VMEM),
        scratch_shapes=[
            pltpu.VMEM((px, rows, lev), F32),
            pltpu.VMEM((px, rows, lev), F32),
            pltpu.SemaphoreType.DMA((elements,)),
        ],
        compiler_params=params(14),
        cost_estimate=cost(64 * MIB, 12 * MIB),
        name="local",
    )(slabs, wind_x, wind_y)

    send_d, send_c = pl.pallas_call(
        edge_kernel,
        out_shape=(struct(nt * px, lev),) * 2,
        in_specs=[VMEM, VMEM, VMEM],
        out_specs=(VMEM, VMEM),
        scratch_shapes=[pltpu.VMEM((8 * px, lev), F32)],
        compiler_params=params(8),
        cost_estimate=cost(MIB, MIB),
        name="edges",
    )(edges, got_b, got_a)
    got_d = lax.ppermute(send_d, "blk", pair_d)
    got_c = lax.ppermute(send_c, "blk", pair_c)

    table, onehots, lanes, costs, first, second, bad = pl.pallas_call(
        gains_kernel,
        out_shape=(
            struct(groups, lev),
            struct(2 * groups, groups, dtype=BF16),
            struct(groups, lev),
            struct(groups, lev),
            struct(2 * lev, 2 * lev, dtype=BF16),
            struct(2 * lev, lev, dtype=BF16),
            struct(8, lev),
        ),
        in_specs=[VMEM] * 4,
        out_specs=(VMEM,) * 7,
        scratch_shapes=[pltpu.VMEM((MAXC, lev), F32)],
        compiler_params=params(8),
        cost_estimate=cost(512 * MIB, MIB),
        name="gains",
    )(mixing, destinations.reshape(1, groups), group_costs.reshape(1, groups), triggers)

    early = pl.pallas_call(
        early_rain_kernel,
        out_shape=struct(groups, lev),
        in_specs=[VMEM] * 4,
        out_specs=VMEM,
        scratch_shapes=[pltpu.VMEM((2, rows, lev), F32)],
        compiler_params=params(8),
        cost_estimate=cost(512 * MIB, MIB),
        name="early_rain",
    )(tracer, got_a, got_b, table)

    outgoing = pl.pallas_call(
        rain_kernel,
        out_shape=struct(groups, lev),
        in_specs=[VMEM] * 13,
        out_specs=VMEM,
        scratch_shapes=[pltpu.VMEM((groups, lev), F32), pltpu.VMEM((2, rows, lev), F32)],
        compiler_params=params(12),
        cost_estimate=cost(64 * MIB, 2 * MIB),
        name="rain",
    )(costs, bad, tracer, got_a, got_b, got_c, got_d, early, table, lanes, onehots, first, second)

    incoming = lax.all_to_all(outgoing, ("elem", "blk"), split_axis=0, concat_axis=0, tiled=True)

    chunks = 4
    new = pl.pallas_call(
        mix_kernel,
        out_shape=struct(px, rows, lev),
        in_specs=[HBM] * 11,
        out_specs=HBM,
        scratch_shapes=[
            pltpu.VMEM((px, rows, lev), F32),
            pltpu.VMEM((px, rows, lev), F32),
            pltpu.VMEM((MAXC, lev, 3 * lev), BF16),
            pltpu.SMEM((groups,), jnp.int32),
            pltpu.VMEM((8, lev), F32),
            pltpu.VMEM((lev, lev), F32),
            pltpu.VMEM((px, py), jnp.int32),
            pltpu.VMEM((rows, lev), F32),
            pltpu.VMEM((rows, lev), F32),
            pltpu.VMEM((nt * px, lev), F32),
            pltpu.VMEM((nt * px, lev), F32),
            pltpu.VMEM((2 * lev, 2 * lev), BF16),
            pltpu.VMEM((2 * lev, lev), BF16),
            pltpu.VMEM((rows, lev), F32),
            pltpu.SemaphoreType.DMA((chunks,)),
            pltpu.SemaphoreType.DMA((2 * chunks,)),
            pltpu.SemaphoreType.DMA((10,)),
        ],
        compiler_params=params(60),
        cost_estimate=cost(4096 * MIB, 10 * MIB),
        name="mix",
    )(group_costs, bad, mixing, triggers, got_a, got_b, got_c, got_d, first, second, kept(local))

    rain = pl.pallas_call(
        gather_kernel,
        out_shape=struct(groups * GROUP_COLS // lev, lev),
        in_specs=[VMEM],
        out_specs=VMEM,
        compiler_params=params(8),
        cost_estimate=cost(MIB, MIB),
        name="gather",
    )(incoming)
    return new.reshape(state.shape), rain.reshape(-1)


def solution(mesh):
    return jax.shard_map(
        body,
        mesh=mesh,
        in_specs=(
            P("elem", "blk", None, None),
            P("elem", "blk", None),
            P("elem", "blk", None),
            P(),
            P("elem", "blk"),
            P(("elem", "blk")),
            P(("elem", "blk")),
        ),
        out_specs=(P("elem", "blk", None, None), P(("elem", "blk"))),
        check_vma=False,
    )
```
